512 devices in a mesh: pipe: 16 (over z, core), expert: 32 (over y, x).
Axes of the slice: x: 4, y: 8, z: 8, core: 2. Of those that a mesh axis runs over, the one named last changes fastest.
Arguments:
- fwd_state: bfloat16 [16, 768, 3584], P('pipe', 'expert'), may hold values from -6 to 6
- bwd_state: bfloat16 [16, 768, 3584], P('pipe', 'expert'), may hold values from -6 to 6
- saved_input: bfloat16 [16, 2, 768, 3584], P('pipe', None, 'expert'), may hold values from -6 to 6
- fwd_route: int32 [16, 2, 768, 1], P('pipe', None, 'expert'), may hold values from 0 to 3; in each aligned block of 24 rows (0 to 23, 24 to 47, ..., all dimensions but the last counted through in order) at most 7 rows name the same one
- bwd_route: int32 [16, 2, 768, 1], P('pipe', None, 'expert'), may hold values from 0 to 3; in each aligned block of 24 rows (0 to 23, 24 to 47, ..., all dimensions but the last counted through in order) at most 7 rows name the same one
- fwd_gate: float32 [16, 2, 768], P('pipe', None, 'expert'), may hold values from 0.3 to 1
- bwd_gate: float32 [16, 2, 768], P('pipe', None, 'expert'), may hold values from 0.3 to 1
- w_gate: bfloat16 [16, 3584, 4096], P('pipe', None, 'expert'), may hold values from -0.09375 to 0.09375
- w_up: bfloat16 [16, 3584, 4096], P('pipe', None, 'expert'), may hold values from -0.09375 to 0.09375
- w_down: bfloat16 [16, 4096, 3584], P('pipe', 'expert'), may hold values from -0.1875 to 0.1875
- norm_gain: float32 [16, 3584], P('pipe'), may hold values from 0.5 to 1.5
Outputs:
- fwd_out: bfloat16 [16, 768, 3584], P('pipe', 'expert')
- bwd_out: bfloat16 [16, 768, 3584], P('pipe', 'expert')
The draws below stay inside these ranges and needn't reach their ends.
Inputs may be any that keep to these rules, and one draw needn't show every extreme that they name: `fwd_route`: in the rows of one device at one rank and step, no expert is named more than 7 times, and one is named exactly 7 times. `bwd_route`: as for fwd_route.
All inputs are finite; a program needn't handle non-finite values.
Results may differ from the reference program's by a relative error of at most 0.0068.
Values may be sent and summed in bfloat16 or wider, within the bound.
A program may use at most 64 MiB of HBM per device.

```python
import math
import jax
import jax.numpy as jnp
import numpy as np
from jax import lax

D = 3584
HID_DEV = 128
EXPERTS = 4
HID = 1024
TOK = 24
CAP = 7
TICKS = 2
TOKENS = 768
N_PIPE = 16
N_EXPERT = 32


def block_scale(own_key, extent, split, smallest, top_value):
    level = 1.0
    for position, blocks in split:
        steps = jax.random.uniform(jax.random.fold_in(jax.random.fold_in(own_key, 6), position), (blocks,), jnp.float32, smallest / len(split), top_value / len(split))
        level = level * jnp.repeat(jnp.exp(steps), extent[position] // blocks).reshape((-1,) + (1,) * (len(extent) - 1 - position))
    return level


def routed_block(stream_key, own, number, rows, count, top, bound, slope):
    ranking = jax.random.permutation(stream_key, count)
    packed, common = portions_of(count, rows * top, bound, slope, True), portions_of(count, rows * top, bound, slope, False)
    places = jnp.arange(count)

    def named(sizes, turn):
        used = int((sizes > 0).sum())
        fixed = max(1, used // 4)
        moved = fixed + (places - fixed + turn * (used - fixed)) % max(1, count - fixed)
        return jnp.zeros((count,), jnp.int32).at[ranking[jnp.where(places < fixed, places, moved)]].set(jnp.asarray(sizes, jnp.int32))

    sizes = jnp.where(number % 4 == 0, named(packed, number // 4), named(common, number - number // 4 - 1))
    mixed = jax.random.permutation(jax.random.fold_in(own, 3), count)
    donor, taker = mixed[0:count // 2 * 2:2], mixed[1:count // 2 * 2:2]
    slack = jnp.minimum(sizes[donor] - 1, bound - sizes[taker]) // 2
    slack = jnp.where((donor == ranking[0]) | (taker == ranking[0]) | (sizes[taker] == 0), 0, jnp.maximum(slack, 0))
    moved = jax.random.randint(jax.random.fold_in(own, 4), (count // 2,), 0, 1 << 20) % (slack + 1)
    sizes = sizes.at[donor].add(-moved).at[taker].add(moved)
    members = jnp.searchsorted(jnp.cumsum(sizes), jnp.arange(rows * top), side="right").astype(jnp.int32)
    grid = members.reshape(top, rows).T
    grid = grid[jax.random.permutation(jax.random.fold_in(own, 1), rows)]
    turn = jax.random.randint(jax.random.fold_in(own, 2), (rows, 1), 0, top)
    return jnp.take_along_axis(grid, (jnp.arange(top)[None, :] + turn) % top, axis=1)


def portions_of(amount, total, bound, lean, full):
    loads = [(1 << 20) // math.isqrt(rank ** lean) + 1 for rank in range(1, amount + 1)]
    largest = bound if full else min(bound, max(-(-total // amount), total * loads[0] // sum(loads)))
    least = 1 if total - largest >= amount - 1 else 0
    given, spare = [largest] + [least] * (amount - 1), total - largest - least * (amount - 1)
    while spare > 0:
        candidates = [i for i in range(1, amount) if given[i] < largest] or [i for i in range(1, amount) if given[i] < bound]
        whole, budget = sum([loads[i] for i in candidates]), spare
        for i in candidates:
            extra = min(bound - given[i], max(1, budget * loads[i] // whole), spare)
            given[i] = given[i] + extra
            spare = spare - extra
    return np.array(given)


def scatter_about(own_key, extent, scale, reach, cuts=(), kind=jnp.bfloat16):
    values = jax.random.normal(own_key, extent, jnp.float32) * scale
    if len(cuts) > 0:
        values = block_scale(own_key, extent, cuts, -0.22, 0.18) * values
    return jnp.clip(values, min=-reach, max=reach).astype(kind)


def setup_inputs(seed: int = 0) -> dict:
    splits = jax.random.split(jax.random.key(seed), 12)
    fwd_state = scatter_about(splits[0], (N_PIPE, TOKENS, D), 1.0, 6.0, ((0, 16), (1, 32)))
    bwd_state = scatter_about(splits[1], (N_PIPE, TOKENS, D), 1.0, 6.0, ((0, 16), (1, 32)))
    saved_input = scatter_about(splits[2], (N_PIPE, TICKS, TOKENS, D), 1.0, 6.0, ((0, 16), (2, 32)))
    fwd_route_keys = jax.random.split(jax.random.fold_in(splits[3], 1), N_PIPE * TICKS * TOKENS // TOK)
    fwd_route_turns = jax.random.permutation(jax.random.fold_in(splits[3], 3), N_PIPE * TICKS * TOKENS // TOK)
    fwd_route = jax.vmap(lambda own, number: routed_block(jax.random.fold_in(splits[3], 2), own, number, TOK, EXPERTS, 1, CAP, 2))(fwd_route_keys, fwd_route_turns).reshape((N_PIPE, TICKS, TOKENS, 1))
    bwd_route_keys = jax.random.split(jax.random.fold_in(splits[4], 1), N_PIPE * TICKS * TOKENS // TOK)
    bwd_route_turns = jax.random.permutation(jax.random.fold_in(splits[4], 3), N_PIPE * TICKS * TOKENS // TOK)
    bwd_route = jax.vmap(lambda own, number: routed_block(jax.random.fold_in(splits[4], 2), own, number, TOK, EXPERTS, 1, CAP, 2))(bwd_route_keys, bwd_route_turns).reshape((N_PIPE, TICKS, TOKENS, 1))
    fwd_gate = jnp.clip(jnp.exp(math.log(1.0) - 1.2039728 * jax.random.uniform(splits[5], (N_PIPE, TICKS, TOKENS), jnp.float32) ** block_scale(splits[5], (N_PIPE, TICKS, TOKENS), ((0, 16), (2, 32)), -0.2, 0.2)), 0.3, 1.0)
    bwd_gate = jnp.clip(jnp.exp(math.log(1.0) - 1.2039728 * jax.random.uniform(splits[6], (N_PIPE, TICKS, TOKENS), jnp.float32) ** block_scale(splits[6], (N_PIPE, TICKS, TOKENS), ((0, 16), (2, 32)), -0.2, 0.2)), 0.3, 1.0)
    w_gate = scatter_about(splits[7], (N_PIPE, D, EXPERTS * HID), D ** -0.5, 0.09375, ((0, 16), (2, 32)))
    w_up = scatter_about(splits[8], (N_PIPE, D, EXPERTS * HID), D ** -0.5, 0.09375, ((0, 16), (2, 32)))
    w_down = scatter_about(splits[9], (N_PIPE, EXPERTS * HID, D), HID ** -0.5, 0.1875, ((0, 16), (1, 32)))
    norm_gain = jnp.clip(1.0 + 0.1 * jax.random.normal(splits[10], (N_PIPE, D), jnp.float32), 0.5, 1.5)
    return dict(fwd_state=fwd_state, bwd_state=bwd_state, saved_input=saved_input, fwd_route=fwd_route, bwd_route=bwd_route, fwd_gate=fwd_gate, bwd_gate=bwd_gate, w_gate=w_gate, w_up=w_up, w_down=w_down, norm_gain=norm_gain)


EPS = 1e-06

def norm_rows(rows, gain):
    raw = rows.astype(jnp.float32)
    scale = jax.lax.rsqrt(lax.optimization_barrier(jnp.mean(raw * raw, axis=-1, keepdims=True)) + EPS)
    return (raw, scale, (raw * scale * gain).astype(jnp.bfloat16))

def slot_index(route):
    hits = (route[:, None] == jnp.arange(EXPERTS, dtype=jnp.int32)[None, :]).astype(jnp.int32)
    before = jnp.cumsum(hits, axis=0) - hits
    return (route * CAP + lax.optimization_barrier(jnp.sum(before * hits, axis=1))).astype(jnp.int32)

def place_rows(index, rows):
    return jnp.zeros((EXPERTS * CAP, D), jnp.bfloat16).at[index].set(rows)

def take_rows(table, index):
    return jnp.take(table, index, axis=0)

def scatter_tokens(route, normed):
    index = jax.vmap(slot_index)(route.reshape(N_EXPERT, TOK))
    slots = jax.vmap(place_rows)(index, normed.reshape(N_EXPERT, TOK, D))
    return (index, slots)

def expert_block(slots, expert_id):
    return slots[:, expert_id * CAP:(expert_id + 1) * CAP].reshape(N_EXPERT * CAP, D)

def gather_tokens(outputs, index):
    joined = jnp.stack(outputs, axis=0).reshape(EXPERTS, N_EXPERT, CAP, D)
    joined = jnp.transpose(joined, (1, 0, 2, 3)).reshape(N_EXPERT, EXPERTS * CAP, D)
    return jax.vmap(take_rows)(joined, index).reshape(N_EXPERT * TOK, D)

def layer_forward(rows, route, weight, gate_w, up_w, down_w, gain):
    shards = N_EXPERT // EXPERTS
    raw, scale, normed = norm_rows(rows, gain)
    index, slots = scatter_tokens(route, normed)
    outputs = []
    for expert_id in range(EXPERTS):
        block = expert_block(slots, expert_id)
        low = expert_id * HID
        gated = jnp.dot(block, gate_w[:, low:low + HID], preferred_element_type=jnp.float32)
        upped = jnp.dot(block, up_w[:, low:low + HID], preferred_element_type=jnp.float32)
        hidden = (gated * jax.nn.sigmoid(gated) * upped).astype(jnp.bfloat16)
        total = jnp.zeros((N_EXPERT * CAP, D), jnp.float32)
        for group in range(shards):
            cols = slice(group * HID_DEV, (group + 1) * HID_DEV)
            piece = jnp.dot(hidden[:, cols], down_w[low + group * HID_DEV:low + (group + 1) * HID_DEV], preferred_element_type=jnp.float32)
            total = total + piece.astype(jnp.bfloat16).astype(jnp.float32)
        outputs.append(total)
    moe = gather_tokens(outputs, index)
    return (raw + weight[:, None] * moe).astype(jnp.bfloat16)

def layer_backward(grad, saved, route, weight, gate_w, up_w, down_w, gain):
    shards = N_EXPERT // EXPERTS
    raw, scale, normed = norm_rows(saved, gain)
    scaled = (weight[:, None] * grad.astype(jnp.float32)).astype(jnp.bfloat16)
    index, slots = scatter_tokens(route, normed)
    index_g, grad_slots = scatter_tokens(route, scaled)
    outputs = []
    for expert_id in range(EXPERTS):
        block = expert_block(slots, expert_id)
        grad_block = expert_block(grad_slots, expert_id)
        low = expert_id * HID
        gate_part = gate_w[:, low:low + HID]
        up_part = up_w[:, low:low + HID]
        gated = jnp.dot(block, gate_part, preferred_element_type=jnp.float32)
        upped = jnp.dot(block, up_part, preferred_element_type=jnp.float32)
        dhidden = jnp.dot(grad_block, down_w[low:low + HID].T, preferred_element_type=jnp.float32)
        sigma = jax.nn.sigmoid(gated)
        dgate = (dhidden * upped * sigma * (1.0 + gated * (1.0 - sigma))).astype(jnp.bfloat16)
        dup = (dhidden * gated * sigma).astype(jnp.bfloat16)
        total = jnp.zeros((N_EXPERT * CAP, D), jnp.float32)
        for group in range(shards):
            cols = slice(group * HID_DEV, (group + 1) * HID_DEV)
            piece = jnp.dot(dgate[:, cols], gate_part[:, cols].T, preferred_element_type=jnp.float32)
            piece = piece + jnp.dot(dup[:, cols], up_part[:, cols].T, preferred_element_type=jnp.float32)
            total = total + piece.astype(jnp.bfloat16).astype(jnp.float32)
        outputs.append(total)
    dnorm = gather_tokens(outputs, index)
    weighted = gain * dnorm
    dinput = scale * weighted - raw * scale * scale * scale * lax.optimization_barrier(jnp.mean(raw * weighted, axis=-1, keepdims=True))
    return (grad.astype(jnp.float32) + dinput).astype(jnp.bfloat16)

def reference(fwd_state, bwd_state, saved_input, fwd_route, bwd_route, fwd_gate, bwd_gate, w_gate, w_up, w_down, norm_gain):
    forward = [fwd_state[rank] for rank in range(N_PIPE)]
    backward = [bwd_state[rank] for rank in range(N_PIPE)]
    empty = jnp.zeros((N_EXPERT * TOK, D), jnp.bfloat16)
    new_forward = forward
    new_backward = backward
    for moment in range(TICKS):
        new_forward = [layer_forward(forward[rank], fwd_route[rank, moment, :, 0], fwd_gate[rank, moment], w_gate[rank], w_up[rank], w_down[rank], norm_gain[rank]) for rank in range(N_PIPE)]
        new_backward = [layer_backward(backward[rank], saved_input[rank, moment], bwd_route[rank, moment, :, 0], bwd_gate[rank, moment], w_gate[rank], w_up[rank], w_down[rank], norm_gain[rank]) for rank in range(N_PIPE)]
        if moment + 1 < TICKS:
            forward = [empty] + new_forward[:-1]
            backward = new_backward[1:] + [empty]
    return (jnp.stack(new_forward, axis=0), jnp.stack(new_backward, axis=0))
```

```python
import functools

import jax
import jax.numpy as jnp
from jax import lax
from jax.experimental import pallas as pl
from jax.experimental.pallas import tpu as pltpu
from jax.sharding import PartitionSpec as P

EPS = 1e-06
NX = 4
PAIR = 2
SLOT = 8
BLK = 2 * SLOT
NT = (((1,), (1,)), ((), ()))


def dot(a, b):
    return jnp.dot(a, b, preferred_element_type=jnp.float32)


def dot_nt(a, b):
    return lax.dot_general(a, b, NT, preferred_element_type=jnp.float32)


def slots_of(route):
    tok = route.shape[0]
    lane = lax.broadcasted_iota(jnp.int32, (tok, 128), 1)
    hits = jnp.where(lane == route, 1.0, 0.0)
    row_i = lax.broadcasted_iota(jnp.int32, (tok, tok), 0)
    col_i = lax.broadcasted_iota(jnp.int32, (tok, tok), 1)
    lower = jnp.where(col_i < row_i, 1.0, 0.0)
    before = dot(lower.astype(jnp.bfloat16), hits.astype(jnp.bfloat16))
    return jnp.sum(before * hits, axis=1, keepdims=True).astype(jnp.int32)


def as_row(col):
    tok = col.shape[0]
    row_i = lax.broadcasted_iota(jnp.int32, (tok, tok), 0)
    col_i = lax.broadcasted_iota(jnp.int32, (tok, tok), 1)
    return jnp.sum(jnp.where(row_i == col_i, col, 0), axis=0, keepdims=True)


def as_col(row):
    tok = row.shape[1]
    row_i = lax.broadcasted_iota(jnp.int32, (tok, tok), 0)
    col_i = lax.broadcasted_iota(jnp.int32, (tok, tok), 1)
    return jnp.sum(jnp.where(row_i == col_i, row, 0.0), axis=1, keepdims=True)


def place(route, slot, rows, shift):
    target = as_row(route * BLK + (slot + shift))
    sub = lax.broadcasted_iota(jnp.int32, (rows, route.shape[0]), 0)
    return jnp.where(sub == target, 1.0, 0.0).astype(jnp.bfloat16)


def pick(route, slot, ny, shift):
    lane = lax.broadcasted_iota(jnp.int32, (route.shape[0], ny * BLK), 1)
    mine = (lane % BLK == slot + shift) & (lane // (BLK * PAIR) == route)
    return jnp.where(mine, 1.0, 0.0).astype(jnp.bfloat16)


def kernel(
    ny, npipe, ct,
    fs, bs, sv, fr, br, fg, bg, gain, wg, wu, wd,
    fo, bo,
    wgu, wdn, mb, m0, m1, nrm, sca, dd, d1, gs, gs1, dh, hs, ab, r0s, r0r, r1s, r1r,
    dn, xf, xb, yf, yb,
    l_sem, ws_sem, wr_sem, ds_sem, dr_sem, rs_sem, rr_sem, ss_sem, sr_sem,
):
    width = wd.shape[1]
    hid = wd.shape[0]
    tok = fs.shape[0]
    tiles = width // ct
    me = lax.axis_index("expert")
    pipe = lax.axis_index("pipe")
    y, x = me // NX, me % NX
    right = y * NX + (x + 1) % NX
    left = y * NX + (x + NX - 1) % NX
    p_next = (pipe + 1) % npipe
    p_prev = (pipe + npipe - 1) % npipe
    mesh_id = pl.DeviceIdType.MESH

    def row_dev(k):
        return ((y + k) % ny) * NX + x

    loads = [
        pltpu.make_async_copy(wg, wgu.at[0, :, pl.ds(0, hid)], l_sem.at[0]),
        pltpu.make_async_copy(wu, wgu.at[0, :, pl.ds(hid, hid)], l_sem.at[1]),
        pltpu.make_async_copy(wd, wdn.at[pl.ds(0, hid)], l_sem.at[2]),
    ]
    for c in loads:
        c.start()

    barrier = pltpu.get_barrier_semaphore()
    for k in range(1, ny):
        pl.semaphore_signal(barrier, inc=1, device_id=(pipe, row_dev(k)), device_id_type=mesh_id)
    for dev in (right, left):
        pl.semaphore_signal(barrier, inc=1, device_id=(pipe, dev), device_id_type=mesh_id)
    for q in (p_next, p_prev):
        pl.semaphore_signal(barrier, inc=1, device_id=(q, me), device_id_type=mesh_id)
    pl.semaphore_wait(barrier, ny - 1 + 4)

    def remote(src, dst, send, recv, dev):
        return pltpu.make_async_remote_copy(
            src_ref=src, dst_ref=dst, send_sem=send, recv_sem=recv,
            device_id=dev, device_id_type=mesh_id,
        )

    def w_copy(i, src, dst, dev):
        return remote(src, dst, ws_sem.at[i], wr_sem.at[i], (pipe, dev))

    half = width // 2
    hh = hid // 2
    w = [
        w_copy(0, wgu.at[0], wgu.at[1], right),
        w_copy(1, wgu.at[0], wgu.at[2], left),
        w_copy(2, wdn.at[pl.ds(0, hid)], wdn.at[pl.ds(hid, hid)], right),
        w_copy(3, wdn.at[pl.ds(0, hid)], wdn.at[pl.ds(2 * hid, hid)], left),
        w_copy(4, wgu.at[1, pl.ds(0, half)], wgu.at[3, pl.ds(0, half)], right),
        w_copy(5, wgu.at[2, pl.ds(half, half)], wgu.at[3, pl.ds(half, half)], left),
        w_copy(6, wdn.at[pl.ds(hid, hh)], wdn.at[pl.ds(3 * hid, hh)], right),
        w_copy(7, wdn.at[pl.ds(2 * hid + hh, hh)], wdn.at[pl.ds(3 * hid + hh, hh)], left),
    ]
    loads[0].wait()
    loads[1].wait()
    w[0].start()
    w[1].start()
    loads[2].wait()
    w[2].start()
    w[3].start()

    order = sorted(range(1, ny), key=lambda k: -min(k, ny - k))

    def scatter(phase, m, d, base):
        for k in order:
            e = ((y + k) % ny) // PAIR
            remote(
                m.at[pl.ds(pl.multiple_of(e * BLK, BLK), BLK)],
                d.at[pl.ds(pl.multiple_of(base + y * BLK, BLK), BLK)],
                ds_sem.at[phase, k], dr_sem.at[phase, k], (pipe, row_dev(k)),
            ).start()
        d[pl.ds(pl.multiple_of(base + y * BLK, BLK), BLK), :] = m[
            pl.ds(pl.multiple_of((y // PAIR) * BLK, BLK), BLK), :
        ]

    def scatter_wait(phase, m, d, base, recv):
        for k in order:
            c = remote(
                m.at[pl.ds(0, BLK)],
                d.at[pl.ds(pl.multiple_of(base + ((y + ny - k) % ny) * BLK, BLK), BLK)],
                ds_sem.at[phase, k], dr_sem.at[phase, k], (pipe, row_dev(k)),
            )
            if recv:
                c.wait_recv()
            else:
                c.wait_send()

    def give_back(t, rs, rr):
        for k in order:
            dst = (y + k) % ny
            remote(rs.at[dst], rr.at[y], rs_sem.at[t, k], rr_sem.at[t, k], (pipe, row_dev(k))).start()
        rr[pl.ds(y, 1)] = rs[pl.ds(y, 1)]

    def give_wait(t, rs, rr, recv):
        for k in order:
            c = remote(
                rs.at[(y + k) % ny], rr.at[(y + ny - k) % ny],
                rs_sem.at[t, k], rr_sem.at[t, k], (pipe, row_dev(k)),
            )
            if recv:
                c.wait_recv()
            else:
                c.wait_send()

    def norm_scale(raw):
        return lax.rsqrt(jnp.mean(raw * raw, axis=-1, keepdims=True) + EPS)

    g = gain[...]
    routes_f = [fr[t] for t in range(2)]
    routes_b = [br[t] for t in range(2)]
    slots_f = [slots_of(r) for r in routes_f]
    slots_b = [slots_of(r) for r in routes_b]
    gates_f = [as_col(fg[pl.ds(t, 1), :]) for t in range(2)]
    gates_b = [as_col(bg[pl.ds(t, 1), :]) for t in range(2)]
    m_rows = m0.shape[0]

    def fill(m, pa, pb):
        def tile(i, carry):
            cols = pl.ds(pl.multiple_of(i * ct, ct), ct)
            m[:, cols] = (dot(pa, nrm[:, cols]) + dot(pb, sca[:, cols])).astype(jnp.bfloat16)
            return carry

        lax.fori_loop(0, tiles, tile, 0)

    raw = fs[...].astype(jnp.float32)
    nrm[...] = (raw * norm_scale(raw) * g).astype(jnp.bfloat16)
    sca[...] = (gates_b[0] * bs[...].astype(jnp.float32)).astype(jnp.bfloat16)
    fill(
        m0,
        place(routes_f[0], slots_f[0], m_rows, 0),
        place(routes_b[0], slots_b[0], m_rows, SLOT),
    )
    scatter(0, m0, dd, 0)
    b_scale = []
    for t, dst in ((0, nrm), (1, sca)):
        raw = sv[t].astype(jnp.float32)
        scale = norm_scale(raw)
        b_scale.append(scale)
        dst[...] = (raw * scale * g).astype(jnp.bfloat16)
    fill(
        mb,
        place(routes_b[0], slots_b[0], m_rows, 0),
        place(routes_b[1], slots_b[1], m_rows, SLOT),
    )
    scatter(1, mb, dd, ny * BLK)

    scatter_wait(0, m0, dd, 0, True)
    scatter_wait(1, mb, dd, ny * BLK, True)

    def into_hidden(q):
        gs[q] = dot(dd[...], wgu[q]).reshape(2 * ny, BLK, 2 * hid)
        dh[q] = dot_nt(dd[pl.ds(0, ny * BLK)], wdn[pl.ds(q * hid, hid)]).reshape(ny, BLK, hid)

    into_hidden(0)
    w[0].wait_recv()
    w[4].start()
    w[1].wait_recv()
    w[5].start()
    w[2].wait_recv()
    w[6].start()
    w[3].wait_recv()
    w[7].start()
    into_hidden(1)
    into_hidden(2)
    for i in (4, 5, 6, 7):
        w[i].wait_recv()
    into_hidden(3)

    rows = ny * SLOT

    def expert_out(t, gf, rs):
        for q in range(NX):
            f = gf[q, pl.ds(0, ny), pl.ds(0, SLOT), :].reshape(rows, 2 * hid)
            gated, upped = f[:, :hid], f[:, hid:]
            hidden = gated * jax.nn.sigmoid(gated) * upped
            hs[:, pl.ds(q * hid, hid)] = hidden.astype(jnp.bfloat16)
            b = gs[q, pl.ds(ny, ny), pl.ds(t * SLOT, SLOT), :].reshape(rows, 2 * hid)
            gated, upped = b[:, :hid], b[:, hid:]
            dhid = dh[q, :, pl.ds(SLOT, SLOT), :].reshape(rows, hid)
            s = jax.nn.sigmoid(gated)
            da = dhid * upped * s * (1.0 + gated * (1.0 - s))
            db = dhid * gated * s
            ab[q, :, pl.ds(0, hid)] = da.astype(jnp.bfloat16)
            ab[q, :, pl.ds(hid, hid)] = db.astype(jnp.bfloat16)

        def tile(i, carry):
            cols = pl.ds(pl.multiple_of(i * ct, ct), ct)
            f = dot(hs[...], wdn[:, cols])
            b = dot_nt(ab[0], wgu[0, cols, :])
            for q in range(1, NX):
                b = b + dot_nt(ab[q], wgu[q, cols, :])
            both = jnp.concatenate(
                [f.reshape(ny, SLOT, ct), b.reshape(ny, SLOT, ct)], axis=1
            )
            rs[:, :, cols] = both.astype(jnp.bfloat16)
            return carry

        lax.fori_loop(0, tiles, tile, 0)

    def finish(t, f_old, b_old, rr, f_out, b_out):
        sel_f = pick(routes_f[t], slots_f[t], ny, 0)
        sel_b = pick(routes_b[t], slots_b[t], ny, SLOT)

        def tile(i, total):
            cols = pl.ds(pl.multiple_of(i * ct, ct), ct)
            back = rr[:, :, cols].reshape(ny * BLK, ct)
            new = f_old[:, cols].astype(jnp.float32) + gates_f[t] * dot(sel_f, back)
            f_out[pl.ds(0, tok), cols] = new.astype(jnp.bfloat16)
            weighted = gain[:, cols] * dot(sel_b, back)
            dn[:, cols] = weighted
            xs = sv[t, :, cols].astype(jnp.float32)
            return total + jnp.sum(xs * weighted, axis=-1, keepdims=True)

        total = lax.fori_loop(0, tiles, tile, jnp.zeros((tok, 1), jnp.float32))
        r = b_scale[t]
        factor = r * r * r * (total * (1.0 / width))

        def tile2(i, carry):
            cols = pl.ds(pl.multiple_of(i * ct, ct), ct)
            xs = sv[t, :, cols].astype(jnp.float32)
            dx = b_old[:, cols].astype(jnp.float32) + (r * dn[:, cols] - xs * factor)
            b_out[pl.ds(0, tok), cols] = dx.astype(jnp.bfloat16)
            return carry

        lax.fori_loop(0, tiles, tile2, 0)

    expert_out(0, gs, r0s)
    give_back(0, r0s, r0r)
    give_wait(0, r0s, r0r, True)
    finish(0, fs, bs, r0r, xf, xb)

    sf = remote(xf, yf, ss_sem.at[0], sr_sem.at[0], (p_next, me))
    sb = remote(xb, yb, ss_sem.at[1], sr_sem.at[1], (p_prev, me))
    sf.start()
    sb.start()
    sf.wait_recv()
    sb.wait_recv()
    keep_f = jnp.where(pipe > 0, 1.0, 0.0)
    keep_b = jnp.where(pipe < npipe - 1, 1.0, 0.0)
    yf[...] = (yf[...].astype(jnp.float32) * keep_f).astype(jnp.bfloat16)
    yb[...] = (yb[...].astype(jnp.float32) * keep_b).astype(jnp.bfloat16)
    f_old = yf.at[pl.ds(0, tok)]
    b_old = yb.at[pl.ds(0, tok)]

    raw = f_old[...].astype(jnp.float32)
    nrm[...] = (raw * norm_scale(raw) * g).astype(jnp.bfloat16)
    sca[...] = (gates_b[1] * b_old[...].astype(jnp.float32)).astype(jnp.bfloat16)
    fill(
        m1,
        place(routes_f[1], slots_f[1], m_rows, 0),
        place(routes_b[1], slots_b[1], m_rows, SLOT),
    )
    scatter(2, m1, d1, 0)
    scatter_wait(2, m1, d1, 0, True)
    for q in range(NX):
        gs1[q] = dot(d1[...], wgu[q]).reshape(ny, BLK, 2 * hid)
        dh[q] = dot_nt(d1[...], wdn[pl.ds(q * hid, hid)]).reshape(ny, BLK, hid)
    expert_out(1, gs1, r1s)
    give_back(1, r1s, r1r)
    give_wait(1, r1s, r1r, True)
    finish(1, f_old, b_old, r1r, fo, bo)

    for c in w:
        c.wait_send()
    scatter_wait(0, m0, dd, 0, False)
    scatter_wait(1, mb, dd, ny * BLK, False)
    scatter_wait(2, m1, d1, 0, False)
    give_wait(0, r0s, r0r, False)
    give_wait(1, r1s, r1r, False)
    sf.wait_send()
    sb.wait_send()


def local(
    n_expert, npipe, fwd_state, bwd_state, saved_input, fwd_route, bwd_route, fwd_gate, bwd_gate,
    w_gate, w_up, w_down, norm_gain,
):
    ny = n_expert // NX
    experts = ny // PAIR
    tok, width = fwd_state.shape[1:]
    hid = w_down.shape[1]
    ct = 512
    pad = -(-tok // 16) * 16
    bf, f32 = jnp.bfloat16, jnp.float32
    vmem = pl.BlockSpec(memory_space=pltpu.VMEM)
    hbm = pl.BlockSpec(memory_space=pl.ANY)
    scratch = [
        pltpu.VMEM((NX, width, 2 * hid), bf),
        pltpu.VMEM((NX * hid, width), bf),
        pltpu.VMEM((experts * BLK, width), bf),
        pltpu.VMEM((experts * BLK, width), bf),
        pltpu.VMEM((experts * BLK, width), bf),
        pltpu.VMEM((tok, width), bf),
        pltpu.VMEM((tok, width), bf),
        pltpu.VMEM((2 * ny * BLK, width), bf),
        pltpu.VMEM((ny * BLK, width), bf),
        pltpu.VMEM((NX, 2 * ny, BLK, 2 * hid), f32),
        pltpu.VMEM((NX, ny, BLK, 2 * hid), f32),
        pltpu.VMEM((NX, ny, BLK, hid), f32),
        pltpu.VMEM((ny * SLOT, NX * hid), bf),
        pltpu.VMEM((NX, ny * SLOT, 2 * hid), bf),
        pltpu.VMEM((ny, BLK, width), bf),
        pltpu.VMEM((ny, BLK, width), bf),
        pltpu.VMEM((ny, BLK, width), bf),
        pltpu.VMEM((ny, BLK, width), bf),
        pltpu.VMEM((tok, width), f32),
        pltpu.VMEM((pad, width), bf),
        pltpu.VMEM((pad, width), bf),
        pltpu.VMEM((pad, width), bf),
        pltpu.VMEM((pad, width), bf),
        pltpu.SemaphoreType.DMA((3,)),
        pltpu.SemaphoreType.DMA((8,)),
        pltpu.SemaphoreType.DMA((8,)),
        pltpu.SemaphoreType.DMA((3, ny)),
        pltpu.SemaphoreType.DMA((3, ny)),
        pltpu.SemaphoreType.DMA((2, ny)),
        pltpu.SemaphoreType.DMA((2, ny)),
        pltpu.SemaphoreType.DMA((2,)),
        pltpu.SemaphoreType.DMA((2,)),
    ]
    fo, bo = pl.pallas_call(
        functools.partial(kernel, ny, npipe, ct),
        out_shape=[jax.ShapeDtypeStruct((tok, width), bf)] * 2,
        in_specs=[vmem] * 8 + [hbm] * 3,
        out_specs=[vmem] * 2,
        scratch_shapes=scratch,
        compiler_params=pltpu.CompilerParams(
            collective_id=0, has_side_effects=True, vmem_limit_bytes=56 << 20
        ),
    )(
        fwd_state[0], bwd_state[0], saved_input[0], fwd_route[0], bwd_route[0],
        fwd_gate[0], bwd_gate[0], norm_gain, w_gate[0], w_up[0], w_down[0],
    )
    return fo[None], bo[None]


def solution(mesh):
    placed = (
        P("pipe", "expert", None),
        P("pipe", "expert", None),
        P("pipe", None, "expert", None),
        P("pipe", None, "expert", None),
        P("pipe", None, "expert", None),
        P("pipe", None, "expert"),
        P("pipe", None, "expert"),
        P("pipe", None, "expert"),
        P("pipe", None, "expert"),
        P("pipe", "expert", None),
        P("pipe", None),
    )
    return jax.shard_map(
        functools.partial(local, mesh.shape["expert"], mesh.shape["pipe"]),
        mesh=mesh,
        in_specs=placed,
        out_specs=(P("pipe", "expert", None), P("pipe", "expert", None)),
        check_vma=False,
    )
```

```python
import functools

import jax
import jax.numpy as jnp
from jax import lax
from jax.experimental import pallas as pl
from jax.experimental.pallas import tpu as pltpu
from jax.sharding import PartitionSpec as P

EPS = 1e-06
NX = 4
PAIR = 2
SLOT = 8
BLK = 2 * SLOT
NT = (((1,), (1,)), ((), ()))


def dot(a, b):
    return jnp.dot(a, b, preferred_element_type=jnp.float32)


def dot_nt(a, b):
    return lax.dot_general(a, b, NT, preferred_element_type=jnp.float32)


def slots_of(route):
    tok = route.shape[0]
    lane = lax.broadcasted_iota(jnp.int32, (tok, 128), 1)
    hits = jnp.where(lane == route, 1.0, 0.0)
    row_i = lax.broadcasted_iota(jnp.int32, (tok, tok), 0)
    col_i = lax.broadcasted_iota(jnp.int32, (tok, tok), 1)
    lower = jnp.where(col_i < row_i, 1.0, 0.0)
    before = dot(lower.astype(jnp.bfloat16), hits.astype(jnp.bfloat16))
    return jnp.sum(before * hits, axis=1, keepdims=True).astype(jnp.int32)


def as_row(col):
    tok = col.shape[0]
    row_i = lax.broadcasted_iota(jnp.int32, (tok, tok), 0)
    col_i = lax.broadcasted_iota(jnp.int32, (tok, tok), 1)
    return jnp.sum(jnp.where(row_i == col_i, col, 0), axis=0, keepdims=True)


def as_col(row):
    tok = row.shape[1]
    row_i = lax.broadcasted_iota(jnp.int32, (tok, tok), 0)
    col_i = lax.broadcasted_iota(jnp.int32, (tok, tok), 1)
    return jnp.sum(jnp.where(row_i == col_i, row, jnp.zeros_like(row)), axis=1, keepdims=True)


def place(route, slot, rows, shift):
    target = as_row(route * BLK + (slot + shift))
    sub = lax.broadcasted_iota(jnp.int32, (rows, route.shape[0]), 0)
    return jnp.where(sub == target, 1.0, 0.0).astype(jnp.bfloat16)


def pick(route, slot, expert_of, shift):
    lane = lax.broadcasted_iota(jnp.int32, (route.shape[0], expert_of.shape[1]), 1)
    mine = (lane % BLK == slot + shift) & (expert_of == route)
    return jnp.where(mine, 1.0, 0.0).astype(jnp.bfloat16)


def kernel(
    ny, npipe, ct,
    fs, bs, sv, fr, br, fg, bg, gain, wg, wu, wd,
    fo, bo,
    wgu, wdn, m0, mb, m1, nrm, sca, dd, d1, gs, gs1, dh, hs, ab, po,
    xs0, xr0, rs0, rr0, xs1, xr1, rs1, rr1, dn, xf, xb, yf, yb,
    l_sem, ws_sem, wr_sem, ds_sem, dr_sem, es_sem, er_sem, cs_sem, cr_sem, rs_sem, rr_sem, ss_sem, sr_sem,
):
    width = wd.shape[1]
    hid = wd.shape[0]
    tok = fs.shape[0]
    tiles = width // ct
    ns = ny // PAIR
    me = lax.axis_index("expert")
    pipe = lax.axis_index("pipe")
    y, x = me // NX, me % NX
    sg = 1 - 2 * (y % 2)
    core = pipe % 2
    p_next = (pipe + 1) % npipe
    p_prev = (pipe + npipe - 1) % npipe
    mesh_id = pl.DeviceIdType.MESH

    def at_row(row):
        return (pipe, ((row + ny) % ny) * NX + x)

    def at_col(col):
        return (pipe, y * NX + (col + NX) % NX)

    def source_row(j):
        return (y - sg * j + ny) % ny

    def target_row(j):
        return (y + (sg * j if j % 2 == 0 else -sg * j) + ny) % ny

    partner = at_row(y + sg)
    across = at_col(x + 2)
    taker = at_col(x + 3 + 2 * core)

    loads = [
        pltpu.make_async_copy(wg, wgu.at[0, :, pl.ds(0, hid)], l_sem.at[0]),
        pltpu.make_async_copy(wu, wgu.at[0, :, pl.ds(hid, hid)], l_sem.at[1]),
        pltpu.make_async_copy(wd, wdn.at[pl.ds(0, hid)], l_sem.at[2]),
    ]
    for c in loads:
        c.start()

    barrier = pltpu.get_barrier_semaphore()
    peers = [at_row(y + k) for k in range(1, ny)] + [at_col(x + k) for k in range(1, NX)]
    peers += [(p_next, me), (p_prev, me)]
    for dev in peers:
        pl.semaphore_signal(barrier, inc=1, device_id=dev, device_id_type=mesh_id)

    def remote(src, dst, send, recv, dev):
        return pltpu.make_async_remote_copy(
            src_ref=src, dst_ref=dst, send_sem=send, recv_sem=recv,
            device_id=dev, device_id_type=mesh_id,
        )

    def part(q, i):
        if i < 4:
            return wgu.at[q, pl.ds(i * (width // 4), width // 4)]
        return wdn.at[pl.ds(q * hid + (i - 4) * (hid // 2), hid // 2)]

    to_partner = [remote(part(0, i), part(2, i), ws_sem.at[i], wr_sem.at[i], partner) for i in range(6)]
    to_taker = [
        remote(wgu.at[0], wgu.at[1], ws_sem.at[6], wr_sem.at[6], taker),
        remote(wdn.at[pl.ds(0, hid)], wdn.at[pl.ds(hid, hid)], ws_sem.at[7], wr_sem.at[7], taker),
    ]
    passed = [remote(part(2, i), part(3, i), ws_sem.at[8 + i], wr_sem.at[8 + i], taker) for i in range(6)]
    far_first = list(range(ns - 1, 0, -1))

    def blk(ref, i):
        start = i * BLK if isinstance(i, int) else pl.multiple_of(i * BLK, BLK)
        return ref.at[pl.ds(start, BLK)]

    def send_copy(phase, m, d, base, j):
        return remote(
            blk(m, target_row(j) // PAIR), blk(d, base + j),
            ds_sem.at[phase, j], dr_sem.at[phase, j], at_row(target_row(j)),
        )

    def pass_copy(phase, d, base, j):
        return remote(
            blk(d, base + j), blk(d, base + ns + j), es_sem.at[phase, j], er_sem.at[phase, j], across
        )

    def scatter(phase, m, d, base):
        for j in far_first:
            send_copy(phase, m, d, base, j).start()
        blk(d, base)[...] = blk(m, y // PAIR)[...]
        pass_copy(phase, d, base, 0).start()

    def scatter_pass(phase, m, d, base):
        for j in range(1, ns):
            send_copy(phase, m, d, base, j).wait_recv()
            pass_copy(phase, d, base, j).start()

    def scatter_end(phase, d, base):
        for j in range(ns):
            pass_copy(phase, d, base, j).wait_recv()

    def norm_scale(raw):
        return lax.rsqrt(jnp.mean(raw * raw, axis=-1, keepdims=True) + EPS)

    g = gain[...]
    routes_f = [as_col(fr[pl.ds(t, 1), :]) for t in range(2)]
    routes_b = [as_col(br[pl.ds(t, 1), :]) for t in range(2)]
    slots_f = [slots_of(r) for r in routes_f]
    slots_b = [slots_of(r) for r in routes_b]
    gates_f = [as_col(fg[pl.ds(t, 1), :]) for t in range(2)]
    gates_b = [as_col(bg[pl.ds(t, 1), :]) for t in range(2)]
    m_rows = m0.shape[0]

    def fill(m, pa, pb):
        def tile(i, carry):
            cols = pl.ds(pl.multiple_of(i * ct, ct), ct)
            m[:, cols] = (dot(pa, nrm[:, cols]) + dot(pb, sca[:, cols])).astype(jnp.bfloat16)
            return carry

        lax.fori_loop(0, tiles, tile, 0)

    raw = fs[...].astype(jnp.float32)
    nrm[...] = (raw * norm_scale(raw) * g).astype(jnp.bfloat16)
    sca[...] = (gates_b[0] * bs[...].astype(jnp.float32)).astype(jnp.bfloat16)
    fill(
        m0,
        place(routes_f[0], slots_f[0], m_rows, 0),
        place(routes_b[0], slots_b[0], m_rows, SLOT),
    )
    pl.semaphore_wait(barrier, len(peers))
    scatter(0, m0, dd, 0)
    loads[0].wait()
    loads[1].wait()
    to_partner[0].start()
    to_taker[0].start()
    b_scale = []
    for t, dst in ((0, nrm), (1, sca)):
        raw = sv[t].astype(jnp.float32)
        scale = norm_scale(raw)
        b_scale.append(scale)
        dst[...] = (raw * scale * g).astype(jnp.bfloat16)
    fill(
        mb,
        place(routes_b[0], slots_b[0], m_rows, 0),
        place(routes_b[1], slots_b[1], m_rows, SLOT),
    )
    scatter(1, mb, dd, ny)
    loads[2].wait()
    for c in to_partner[1:]:
        c.start()
    scatter_pass(0, m0, dd, 0)
    scatter_pass(1, mb, dd, ny)
    to_taker[1].start()

    def into_hidden(q):
        gs[q] = dot(dd[...], wgu[q]).reshape(2 * ny, BLK, 2 * hid)
        dh[q] = dot_nt(dd[pl.ds(0, ny * BLK)], wdn[pl.ds(q * hid, hid)]).reshape(ny, BLK, hid)

    for i in range(2):
        to_partner[i].wait_recv()
        passed[i].start()
    scatter_end(0, dd, 0)
    scatter_end(1, dd, ny)
    into_hidden(0)
    for i in range(2, 4):
        to_partner[i].wait_recv()
        passed[i].start()
    for c in to_taker:
        c.wait_recv()
    into_hidden(1)
    for i in range(4, 6):
        to_partner[i].wait_recv()
        passed[i].start()
    into_hidden(2)
    for c in passed:
        c.wait_recv()
    into_hidden(3)

    rows = ny * SLOT

    def expert_out(t, gf, xs):
        for q in range(NX):
            f = gf[q, pl.ds(0, ny), pl.ds(0, SLOT), :].reshape(rows, 2 * hid)
            gated, upped = f[:, :hid], f[:, hid:]
            hidden = gated * jax.nn.sigmoid(gated) * upped
            hs[:, pl.ds(q * hid, hid)] = hidden.astype(jnp.bfloat16)
            b = gs[q, pl.ds(ny, ny), pl.ds(t * SLOT, SLOT), :].reshape(rows, 2 * hid)
            gated, upped = b[:, :hid], b[:, hid:]
            dhid = dh[q, :, pl.ds(SLOT, SLOT), :].reshape(rows, hid)
            s = jax.nn.sigmoid(gated)
            da = dhid * upped * s * (1.0 + gated * (1.0 - s))
            db = dhid * gated * s
            ab[q, :, pl.ds(0, hid)] = da.astype(jnp.bfloat16)
            ab[q, :, pl.ds(hid, hid)] = db.astype(jnp.bfloat16)

        def tile(i, carry):
            cols = pl.ds(pl.multiple_of(i * ct, ct), ct)
            f = dot(hs[...], wdn[:, cols])
            b = dot_nt(ab[0], wgu[0, cols, :])
            for q in range(1, NX):
                b = b + dot_nt(ab[q], wgu[q, cols, :])
            both = jnp.concatenate(
                [f.reshape(ny, SLOT, ct), b.reshape(ny, SLOT, ct)], axis=1
            )
            po[:, :, cols] = both[:ns]
            xs[:, :, cols] = both[ns:].astype(jnp.bfloat16)
            return carry

        lax.fori_loop(0, tiles, tile, 0)

    def half_copy(t, xs, xr, j):
        return remote(xs.at[j], xr.at[j], cs_sem.at[t, j], cr_sem.at[t, j], across)

    def back_copy(t, rs, rr, j):
        return remote(rs.at[j], rr.at[j], rs_sem.at[t, j], rr_sem.at[t, j], at_row(source_row(j)))

    def give_back(t, xs, xr, rs, rr):
        for j in far_first + [0]:
            half_copy(t, xs, xr, j).start()
        for j in far_first + [0]:
            half_copy(t, xs, xr, j).wait_recv()
            (rs if j else rr)[j] = (po[j] + xr[j].astype(jnp.float32)).astype(jnp.bfloat16)
            if j:
                back_copy(t, rs, rr, j).start()
        for j in range(1, ns):
            remote(
                rs.at[j], rr.at[j], rs_sem.at[t, j], rr_sem.at[t, j], at_row(target_row(j))
            ).wait_recv()

    jb = lax.broadcasted_iota(jnp.int32, (tok, ns * BLK), 1) // BLK
    step = jnp.where(jb % 2 == 0, jb, -jb) * sg
    expert_of = ((y + step + ny) % ny) // PAIR

    def finish(t, f_old, b_old, rr, f_out, b_out, after_f=None):
        sel_f = pick(routes_f[t], slots_f[t], expert_of, 0)
        sel_b = pick(routes_b[t], slots_b[t], expert_of, SLOT)

        def tile(i, total):
            cols = pl.ds(pl.multiple_of(i * ct, ct), ct)
            back = rr[:, :, cols].reshape(ns * BLK, ct)
            new = f_old[:, cols].astype(jnp.float32) + gates_f[t] * dot(sel_f, back)
            f_out[pl.ds(0, tok), cols] = new.astype(jnp.bfloat16)
            weighted = gain[:, cols] * dot(sel_b, back)
            dn[:, cols] = weighted
            xs = sv[t, :, cols].astype(jnp.float32)
            return total + jnp.sum(xs * weighted, axis=-1, keepdims=True)

        total = lax.fori_loop(0, tiles, tile, jnp.zeros((tok, 1), jnp.float32))
        if after_f is not None:
            after_f()
        r = b_scale[t]
        factor = r * r * r * (total * (1.0 / width))

        def tile2(i, carry):
            cols = pl.ds(pl.multiple_of(i * ct, ct), ct)
            xs = sv[t, :, cols].astype(jnp.float32)
            dx = b_old[:, cols].astype(jnp.float32) + (r * dn[:, cols] - xs * factor)
            b_out[pl.ds(0, tok), cols] = dx.astype(jnp.bfloat16)
            return carry

        lax.fori_loop(0, tiles, tile2, 0)

    expert_out(0, gs, xs0)
    give_back(0, xs0, xr0, rs0, rr0)

    sf = remote(xf, yf, ss_sem.at[0], sr_sem.at[0], (p_next, me))
    sb = remote(xb, yb, ss_sem.at[1], sr_sem.at[1], (p_prev, me))
    finish(0, fs, bs, rr0, xf, xb, sf.start)
    sb.start()
    sf.wait_recv()
    keep_f = jnp.where(pipe > 0, 1.0, 0.0)
    keep_b = jnp.where(pipe < npipe - 1, 1.0, 0.0)
    yf[...] = (yf[...].astype(jnp.float32) * keep_f).astype(jnp.bfloat16)
    f_old = yf.at[pl.ds(0, tok)]
    b_old = yb.at[pl.ds(0, tok)]

    raw = f_old[...].astype(jnp.float32)
    nrm[...] = (raw * norm_scale(raw) * g).astype(jnp.bfloat16)
    sb.wait_recv()
    yb[...] = (yb[...].astype(jnp.float32) * keep_b).astype(jnp.bfloat16)
    sca[...] = (gates_b[1] * b_old[...].astype(jnp.float32)).astype(jnp.bfloat16)
    fill(
        m1,
        place(routes_f[1], slots_f[1], m_rows, 0),
        place(routes_b[1], slots_b[1], m_rows, SLOT),
    )
    scatter(2, m1, d1, 0)
    scatter_pass(2, m1, d1, 0)
    scatter_end(2, d1, 0)
    for q in range(NX):
        gs1[q] = dot(d1[...], wgu[q]).reshape(ny, BLK, 2 * hid)
        dh[q] = dot_nt(d1[...], wdn[pl.ds(q * hid, hid)]).reshape(ny, BLK, hid)
    expert_out(1, gs1, xs1)
    give_back(1, xs1, xr1, rs1, rr1)
    finish(1, f_old, b_old, rr1, fo, bo)

    for c in to_partner + to_taker + passed:
        c.wait_send()
    for phase, m, d, base in ((0, m0, dd, 0), (1, mb, dd, ny), (2, m1, d1, 0)):
        for j in range(ns):
            if j:
                send_copy(phase, m, d, base, j).wait_send()
            pass_copy(phase, d, base, j).wait_send()
    for t, xs, xr, rs, rr in ((0, xs0, xr0, rs0, rr0), (1, xs1, xr1, rs1, rr1)):
        for j in range(ns):
            half_copy(t, xs, xr, j).wait_send()
            if j:
                back_copy(t, rs, rr, j).wait_send()
    sf.wait_send()
    sb.wait_send()


def local(
    n_expert, npipe, fwd_state, bwd_state, saved_input, fwd_route, bwd_route, fwd_gate, bwd_gate,
    w_gate, w_up, w_down, norm_gain,
):
    ny = n_expert // NX
    experts = ny // PAIR
    tok, width = fwd_state.shape[1:]
    hid = w_down.shape[1]
    ct = 512
    pad = -(-tok // 16) * 16
    bf, f32 = jnp.bfloat16, jnp.float32
    vmem = pl.BlockSpec(memory_space=pltpu.VMEM)
    hbm = pl.BlockSpec(memory_space=pl.ANY)
    ns = ny // PAIR
    scratch = [
        pltpu.VMEM((NX, width, 2 * hid), bf),
        pltpu.VMEM((NX * hid, width), bf),
        pltpu.VMEM((experts * BLK, width), bf),
        pltpu.VMEM((experts * BLK, width), bf),
        pltpu.VMEM((experts * BLK, width), bf),
        pltpu.VMEM((tok, width), bf),
        pltpu.VMEM((tok, width), bf),
        pltpu.VMEM((2 * ny * BLK, width), bf),
        pltpu.VMEM((ny * BLK, width), bf),
        pltpu.VMEM((NX, 2 * ny, BLK, 2 * hid), f32),
        pltpu.VMEM((NX, ny, BLK, 2 * hid), f32),
        pltpu.VMEM((NX, ny, BLK, hid), f32),
        pltpu.VMEM((ny * SLOT, NX * hid), bf),
        pltpu.VMEM((NX, ny * SLOT, 2 * hid), bf),
        pltpu.VMEM((ns, BLK, width), f32),
    ]
    scratch += [pltpu.VMEM((ns, BLK, width), bf)] * 8
    scratch += [
        pltpu.VMEM((tok, width), f32),
        pltpu.VMEM((pad, width), bf),
        pltpu.VMEM((pad, width), bf),
        pltpu.VMEM((pad, width), bf),
        pltpu.VMEM((pad, width), bf),
    ]
    scratch += [
        pltpu.SemaphoreType.DMA(shape)
        for shape in (
            (3,), (14,), (14,), (3, ns), (3, ns), (3, ns), (3, ns), (2, ns), (2, ns), (2, ns), (2, ns),
            (2,), (2,),
        )
    ]
    fo, bo = pl.pallas_call(
        functools.partial(kernel, ny, npipe, ct),
        out_shape=[jax.ShapeDtypeStruct((tok, width), bf)] * 2,
        in_specs=[vmem] * 8 + [hbm] * 3,
        out_specs=[vmem] * 2,
        scratch_shapes=scratch,
        compiler_params=pltpu.CompilerParams(
            collective_id=0, has_side_effects=True, vmem_limit_bytes=56 << 20
        ),
    )(
        fwd_state[0], bwd_state[0], saved_input[0], fwd_route.reshape(2, tok), bwd_route.reshape(2, tok),
        fwd_gate[0], bwd_gate[0], norm_gain, w_gate[0], w_up[0], w_down[0],
    )
    return fo[None], bo[None]


def solution(mesh):
    placed = (
        P("pipe", "expert", None),
        P("pipe", "expert", None),
        P("pipe", None, "expert", None),
        P("pipe", None, "expert", None),
        P("pipe", None, "expert", None),
        P("pipe", None, "expert"),
        P("pipe", None, "expert"),
        P("pipe", None, "expert"),
        P("pipe", None, "expert"),
        P("pipe", "expert", None),
        P("pipe", None),
    )
    return jax.shard_map(
        functools.partial(local, mesh.shape["expert"], mesh.shape["pipe"]),
        mesh=mesh,
        in_specs=placed,
        out_specs=(P("pipe", "expert", None), P("pipe", "expert", None)),
        check_vma=False,
    )
```

```python
import functools

import jax
import jax.numpy as jnp
from jax import lax
from jax.experimental import pallas as pl
from jax.experimental.pallas import tpu as pltpu
from jax.sharding import PartitionSpec as P

EPS = 1e-06
NX = 4
PAIR = 2
SLOT = 8
BLK = 2 * SLOT
NT = (((1,), (1,)), ((), ()))


def dot(a, b):
    return jnp.dot(a, b, preferred_element_type=jnp.float32)


def dot_nt(a, b):
    return lax.dot_general(a, b, NT, preferred_element_type=jnp.float32)


def slots_of(route):
    tok = route.shape[0]
    lane = lax.broadcasted_iota(jnp.int32, (tok, 128), 1)
    hits = jnp.where(lane == route, 1.0, 0.0)
    row_i = lax.broadcasted_iota(jnp.int32, (tok, tok), 0)
    col_i = lax.broadcasted_iota(jnp.int32, (tok, tok), 1)
    lower = jnp.where(col_i < row_i, 1.0, 0.0)
    before = dot(lower.astype(jnp.bfloat16), hits.astype(jnp.bfloat16))
    return jnp.sum(before * hits, axis=1, keepdims=True).astype(jnp.int32)


def as_row(col):
    tok = col.shape[0]
    row_i = lax.broadcasted_iota(jnp.int32, (tok, tok), 0)
    col_i = lax.broadcasted_iota(jnp.int32, (tok, tok), 1)
    return jnp.sum(jnp.where(row_i == col_i, col, 0), axis=0, keepdims=True)


def as_col(row):
    tok = row.shape[1]
    row_i = lax.broadcasted_iota(jnp.int32, (tok, tok), 0)
    col_i = lax.broadcasted_iota(jnp.int32, (tok, tok), 1)
    return jnp.sum(jnp.where(row_i == col_i, row, jnp.zeros_like(row)), axis=1, keepdims=True)


def place(route, slot, rows, shift):
    target = as_row(route * BLK + (slot + shift))
    sub = lax.broadcasted_iota(jnp.int32, (rows, route.shape[0]), 0)
    return jnp.where(sub == target, 1.0, 0.0).astype(jnp.bfloat16)


def pick(route, slot, expert_of, shift):
    lane = lax.broadcasted_iota(jnp.int32, (route.shape[0], expert_of.shape[1]), 1)
    mine = (lane % BLK == slot + shift) & (expert_of == route)
    return jnp.where(mine, 1.0, 0.0).astype(jnp.bfloat16)


def kernel(
    ny, npipe, ct,
    fs, bs, sv, fr, br, fg, bg, gain, wg, wu, wd,
    fo, bo,
    wgu, wdn, mm, rows_in, dd, gs, dh, hs, ab, po, xs, xr, rs, rr, dn, xf, xb, yf, yb,
    l_sem, ws_sem, wr_sem, ds_sem, dr_sem, es_sem, er_sem, cs_sem, cr_sem, rs_sem, rr_sem, ss_sem, sr_sem,
):
    width = wd.shape[1]
    hid = wd.shape[0]
    tok = fs.shape[0]
    half = width // 2
    tiles = half // ct
    groups = ny // PAIR
    ns = ny // PAIR
    me = lax.axis_index("expert")
    pipe = lax.axis_index("pipe")
    y, x = me // NX, me % NX
    sg = 1 - 2 * (y % 2)
    core = pipe % 2
    p_next = (pipe + 1) % npipe
    p_prev = (pipe + npipe - 1) % npipe
    mesh_id = pl.DeviceIdType.MESH

    def at_row(row):
        return (pipe, ((row + ny) % ny) * NX + x)

    def at_col(col):
        return (pipe, y * NX + (col + NX) % NX)

    def source_row(j):
        return (y - sg * j + ny) % ny

    def target_row(j):
        return (y + (sg * j if j % 2 == 0 else -sg * j) + ny) % ny

    partner = at_row(y + sg)
    across = at_col(x + 2)
    taker = at_col(x + 3 + 2 * core)

    loads = [
        pltpu.make_async_copy(wg, wgu.at[0, :, pl.ds(0, hid)], l_sem.at[0]),
        pltpu.make_async_copy(wu, wgu.at[0, :, pl.ds(hid, hid)], l_sem.at[1]),
        pltpu.make_async_copy(wd, wdn.at[pl.ds(0, hid)], l_sem.at[2]),
    ]
    for c in loads:
        c.start()

    barrier = pltpu.get_barrier_semaphore()
    peers = [at_row(y + k) for k in range(1, ny)] + [at_col(x + k) for k in range(1, NX)]
    peers += [(p_next, me), (p_prev, me)]
    for dev in peers:
        pl.semaphore_signal(barrier, inc=1, device_id=dev, device_id_type=mesh_id)

    def remote(src, dst, send, recv, dev):
        return pltpu.make_async_remote_copy(
            src_ref=src, dst_ref=dst, send_sem=send, recv_sem=recv,
            device_id=dev, device_id_type=mesh_id,
        )

    def part(q, i):
        if i < 4:
            return wgu.at[q, pl.ds(i * (width // 4), width // 4)]
        return wdn.at[pl.ds(q * hid + (i - 4) * (hid // 4), hid // 4)]

    to_partner = [remote(part(0, i), part(2, i), ws_sem.at[i], wr_sem.at[i], partner) for i in range(8)]
    to_taker = [
        remote(wgu.at[0], wgu.at[1], ws_sem.at[16], wr_sem.at[16], taker),
        remote(wdn.at[pl.ds(0, hid)], wdn.at[pl.ds(hid, hid)], ws_sem.at[17], wr_sem.at[17], taker),
    ]
    passed = [remote(part(2, i), part(3, i), ws_sem.at[8 + i], wr_sem.at[8 + i], taker) for i in range(8)]
    far_first = list(range(ns - 1, 0, -1))

    def blk(ref, i):
        start = i * BLK if isinstance(i, int) else pl.multiple_of(i * BLK, BLK)
        return ref.at[pl.ds(start, BLK)]

    def send_copy(kind, j):
        return remote(
            blk(mm, kind * groups + target_row(j) // PAIR), blk(dd, kind * ny + j),
            ds_sem.at[kind, j], dr_sem.at[kind, j], at_row(target_row(j)),
        )

    def pass_copy(kind, j):
        return remote(
            blk(dd, kind * ny + j), blk(dd, kind * ny + ns + j),
            es_sem.at[kind, j], er_sem.at[kind, j], across,
        )

    def scatter(kind):
        for j in far_first:
            send_copy(kind, j).start()
        blk(dd, kind * ny)[...] = blk(mm, kind * groups + y // PAIR)[...]
        pass_copy(kind, 0).start()

    def scatter_pass(kind):
        for j in range(1, ns):
            send_copy(kind, j).wait_recv()
            pass_copy(kind, j).start()

    def scatter_end(kind):
        for j in range(ns):
            pass_copy(kind, j).wait_recv()

    def norm_scale(raw):
        return lax.rsqrt(jnp.mean(raw * raw, axis=-1, keepdims=True) + EPS)

    g = gain[...]
    routes_f = [as_col(fr[pl.ds(t, 1), :]) for t in range(2)]
    routes_b = [as_col(br[pl.ds(t, 1), :]) for t in range(2)]
    slots_f = [slots_of(r) for r in routes_f]
    slots_b = [slots_of(r) for r in routes_b]
    gates_f = [as_col(fg[pl.ds(t, 1), :]) for t in range(2)]
    gates_b = [as_col(bg[pl.ds(t, 1), :]) for t in range(2)]

    def fill(kind, route, slot, values):
        rows_in[...] = values.astype(jnp.bfloat16)
        lo = place(route, slot, groups * BLK, 0)
        hi = place(route, slot, groups * BLK, SLOT)

        def tile(i, carry):
            start = pl.multiple_of(i * ct, ct)
            cols = pl.ds(start, ct)
            cols2 = pl.ds(pl.multiple_of(half + start, 128), ct)
            both = dot(lo, rows_in[:, cols]) + dot(hi, rows_in[:, cols2])
            mm[pl.ds(kind * groups * BLK, groups * BLK), cols] = both.astype(jnp.bfloat16)
            return carry

        lax.fori_loop(0, tiles, tile, 0)

    def fill_tokens(kind, t, state):
        raw = state[...].astype(jnp.float32)
        fill(kind, routes_f[t], slots_f[t], raw * norm_scale(raw) * g)

    def fill_grads(kind, t, state):
        fill(kind, routes_b[t], slots_b[t], gates_b[t] * state[...].astype(jnp.float32))

    def fill_saved(kind, t):
        raw = sv[t].astype(jnp.float32)
        scale = norm_scale(raw)
        fill(kind, routes_b[t], slots_b[t], raw * scale * g)
        return scale

    fill_tokens(0, 0, fs)
    pl.semaphore_wait(barrier, len(peers))
    scatter(0)
    loads[0].wait()
    loads[1].wait()
    to_partner[0].start()
    to_taker[0].start()
    fill_grads(2, 0, bs)
    scatter(2)
    b_scale = [fill_saved(1, 0)]
    scatter(1)
    loads[2].wait()
    for c in to_partner[1:]:
        c.start()
    b_scale.append(fill_saved(3, 1))
    for kind in (0, 2, 1):
        scatter_pass(kind)
    to_taker[1].start()
    for j in far_first:
        send_copy(3, j).start()
    blk(dd, 3 * ny)[...] = blk(mm, 3 * groups + y // PAIR)[...]

    def folded(kind, count, product, w_lo, w_hi):
        a = dd[pl.ds(kind * ny * BLK, count * ny * BLK)]
        lo = product(a, w_lo).reshape(count * ny, BLK, -1)[:, :SLOT]
        hi = product(a, w_hi).reshape(count * ny, BLK, -1)[:, SLOT:]
        return lo + hi

    def through_up(q, kind, count, at):
        gs[q, pl.ds(at * ny, count * ny)] = folded(
            kind, count, dot, wgu[q, pl.ds(0, half)], wgu[q, pl.ds(half, half)]
        )

    def through_down(q, kind, t):
        w_q = wdn.at[pl.ds(q * hid, hid)]
        dh[q, pl.ds(t * ny, ny)] = folded(
            kind, 1, dot_nt, w_q[:, pl.ds(0, half)], w_q[:, pl.ds(half, half)]
        )

    def into_hidden(q):
        through_up(q, 0, 2, 0)
        through_down(q, 2, 0)

    for i in range(2):
        to_partner[i].wait_recv()
        passed[i].start()
    for kind in (0, 2, 1):
        scatter_end(kind)
    into_hidden(0)
    for i in range(2, 4):
        to_partner[i].wait_recv()
        passed[i].start()
    for c in to_taker:
        c.wait_recv()
    into_hidden(1)
    for i in range(4, 8):
        to_partner[i].wait_recv()
        passed[i].start()
    into_hidden(2)
    for c in passed:
        c.wait_recv()
    into_hidden(3)

    rows = ny * SLOT

    def put_out(c, i, lo, hi):
        cols = pl.ds(pl.multiple_of(i * ct, ct), ct)
        both = jnp.concatenate([lo.reshape(ny, SLOT, ct), hi.reshape(ny, SLOT, ct)], axis=1)
        po[c % 2, :, :, cols] = both[:ns]
        xs[c, :, :, cols] = both[ns:].astype(jnp.bfloat16)

    def out_f(t, at):
        for q in range(NX):
            f = gs[q, pl.ds(at * ny, ny)].reshape(rows, 2 * hid)
            gated, upped = f[:, :hid], f[:, hid:]
            hidden = gated * jax.nn.sigmoid(gated) * upped
            hs[:, pl.ds(q * hid, hid)] = hidden.astype(jnp.bfloat16)

        def tile(i, carry):
            start = pl.multiple_of(i * ct, ct)
            lo = dot(hs[...], wdn[:, pl.ds(start, ct)])
            hi = dot(hs[...], wdn[:, pl.ds(pl.multiple_of(half + start, 128), ct)])
            put_out(2 * t, i, lo, hi)
            return carry

        lax.fori_loop(0, tiles, tile, 0)
        half_start(2 * t)

    def out_b(t, at):
        for q in range(NX):
            b = gs[q, pl.ds(at * ny, ny)].reshape(rows, 2 * hid)
            gated, upped = b[:, :hid], b[:, hid:]
            dhid = dh[q, pl.ds(t * ny, ny)].reshape(rows, hid)
            s = jax.nn.sigmoid(gated)
            da = dhid * upped * s * (1.0 + gated * (1.0 - s))
            db = dhid * gated * s
            ab[q, :, pl.ds(0, hid)] = da.astype(jnp.bfloat16)
            ab[q, :, pl.ds(hid, hid)] = db.astype(jnp.bfloat16)

        def through(start):
            b = dot_nt(ab[0], wgu[0, pl.ds(start, ct), :])
            for q in range(1, NX):
                b = b + dot_nt(ab[q], wgu[q, pl.ds(start, ct), :])
            return b

        def tile(i, carry):
            start = pl.multiple_of(i * ct, ct)
            put_out(2 * t + 1, i, through(start), through(pl.multiple_of(half + start, 128)))
            return carry

        lax.fori_loop(0, tiles, tile, 0)
        half_start(2 * t + 1)

    def half_copy(c, j):
        return remote(xs.at[c, j], xr.at[c, j], cs_sem.at[c, j], cr_sem.at[c, j], across)

    def back_copy(c, j):
        return remote(rs.at[c, j], rr.at[c, j], rs_sem.at[c, j], rr_sem.at[c, j], at_row(source_row(j)))

    def half_start(c):
        for j in far_first + [0]:
            half_copy(c, j).start()

    def back_start(c):
        for j in far_first + [0]:
            half_copy(c, j).wait_recv()
            (rs if j else rr)[c, j] = (po[c % 2, j] + xr[c, j].astype(jnp.float32)).astype(jnp.bfloat16)
            if j:
                back_copy(c, j).start()

    def back_wait(c):
        for j in range(1, ns):
            back_copy(c, j).wait_recv()

    jb = lax.broadcasted_iota(jnp.int32, (tok, ns * BLK), 1) // BLK
    step = jnp.where(jb % 2 == 0, jb, -jb) * sg
    expert_of = ((y + step + ny) % ny) // PAIR

    def both_halves(i):
        start = pl.multiple_of(i * ct, ct)
        return pl.ds(start, ct), (pl.ds(start, ct), pl.ds(pl.multiple_of(half + start, 128), ct))

    def finish_f(t, old, out):
        sel = [pick(routes_f[t], slots_f[t], expert_of, shift) for shift in (0, SLOT)]

        def tile(i, carry):
            cols, wide = both_halves(i)
            back = rr[2 * t, :, :, cols].reshape(ns * BLK, ct)
            for s, w in zip(sel, wide):
                new = old[:, w].astype(jnp.float32) + gates_f[t] * dot(s, back)
                out[pl.ds(0, tok), w] = new.astype(jnp.bfloat16)
            return carry

        lax.fori_loop(0, tiles, tile, 0)

    def finish_b(t, old, out):
        sel = [pick(routes_b[t], slots_b[t], expert_of, shift) for shift in (0, SLOT)]

        def tile(i, total):
            cols, wide = both_halves(i)
            back = rr[2 * t + 1, :, :, cols].reshape(ns * BLK, ct)
            for s, w in zip(sel, wide):
                weighted = gain[:, w] * dot(s, back)
                dn[:, w] = weighted
                total = total + jnp.sum(
                    sv[t, :, w].astype(jnp.float32) * weighted, axis=-1, keepdims=True
                )
            return total

        total = lax.fori_loop(0, tiles, tile, jnp.zeros((tok, 1), jnp.float32))
        r = b_scale[t]
        factor = r * r * r * (total * (1.0 / width))

        def tile2(i, carry):
            for w in both_halves(i)[1]:
                saved = sv[t, :, w].astype(jnp.float32)
                dx = old[:, w].astype(jnp.float32) + (r * dn[:, w] - saved * factor)
                out[pl.ds(0, tok), w] = dx.astype(jnp.bfloat16)
            return carry

        lax.fori_loop(0, tiles, tile2, 0)

    out_f(0, 0)
    out_b(0, 1)
    back_start(0)
    back_start(1)
    pass_copy(3, 0).start()
    scatter_pass(3)

    sf = remote(xf, yf, ss_sem.at[0], sr_sem.at[0], (p_next, me))
    sb = remote(xb, yb, ss_sem.at[1], sr_sem.at[1], (p_prev, me))
    back_wait(0)
    finish_f(0, fs, xf)
    sf.start()
    back_wait(1)
    finish_b(0, bs, xb)
    sb.start()
    scatter_end(3)
    for q in range(NX):
        through_up(q, 3, 1, 2)
    keep_f = jnp.where(pipe > 0, 1.0, 0.0)
    keep_b = jnp.where(pipe < npipe - 1, 1.0, 0.0)
    f_old = yf.at[pl.ds(0, tok)]
    b_old = yb.at[pl.ds(0, tok)]

    sf.wait_recv()
    yf[...] = (yf[...].astype(jnp.float32) * keep_f).astype(jnp.bfloat16)
    fill_tokens(4, 1, f_old)
    scatter(4)
    sb.wait_recv()
    yb[...] = (yb[...].astype(jnp.float32) * keep_b).astype(jnp.bfloat16)
    fill_grads(5, 1, b_old)
    scatter(5)
    scatter_pass(4)
    scatter_pass(5)
    scatter_end(4)
    for q in range(NX):
        through_up(q, 4, 1, 3)
    out_f(1, 3)
    scatter_end(5)
    for q in range(NX):
        through_down(q, 5, 1)
    out_b(1, 2)
    back_start(2)
    back_start(3)
    back_wait(2)
    finish_f(1, f_old, fo)
    back_wait(3)
    finish_b(1, b_old, bo)

    for c in to_partner + to_taker + passed:
        c.wait_send()
    for kind in range(6):
        for j in range(ns):
            if j:
                send_copy(kind, j).wait_send()
            pass_copy(kind, j).wait_send()
    for c in range(4):
        for j in range(ns):
            half_copy(c, j).wait_send()
            if j:
                back_copy(c, j).wait_send()
    sf.wait_send()
    sb.wait_send()


def local(
    n_expert, npipe, fwd_state, bwd_state, saved_input, fwd_route, bwd_route, fwd_gate, bwd_gate,
    w_gate, w_up, w_down, norm_gain,
):
    ny = n_expert // NX
    experts = ny // PAIR
    tok, width = fwd_state.shape[1:]
    hid = w_down.shape[1]
    ct = 256
    pad = -(-tok // 16) * 16
    bf, f32 = jnp.bfloat16, jnp.float32
    vmem = pl.BlockSpec(memory_space=pltpu.VMEM)
    hbm = pl.BlockSpec(memory_space=pl.ANY)
    ns = ny // PAIR
    scratch = [
        pltpu.VMEM((NX, width, 2 * hid), bf),
        pltpu.VMEM((NX * hid, width), bf),
        pltpu.VMEM((6 * experts * BLK, width // 2), bf),
        pltpu.VMEM((tok, width), bf),
        pltpu.VMEM((6 * ny * BLK, width // 2), bf),
        pltpu.VMEM((NX, 4 * ny, SLOT, 2 * hid), f32),
        pltpu.VMEM((NX, 2 * ny, SLOT, hid), f32),
        pltpu.VMEM((ny * SLOT, NX * hid), bf),
        pltpu.VMEM((NX, ny * SLOT, 2 * hid), bf),
        pltpu.VMEM((2, ns, BLK, width // 2), f32),
    ]
    scratch += [pltpu.VMEM((4, ns, BLK, width // 2), bf)] * 4
    scratch += [
        pltpu.VMEM((tok, width), f32),
        pltpu.VMEM((pad, width), bf),
        pltpu.VMEM((pad, width), bf),
        pltpu.VMEM((pad, width), bf),
        pltpu.VMEM((pad, width), bf),
    ]
    scratch += [
        pltpu.SemaphoreType.DMA(shape)
        for shape in (
            (3,), (18,), (18,), (6, ns), (6, ns), (6, ns), (6, ns), (4, ns), (4, ns), (4, ns), (4, ns),
            (2,), (2,),
        )
    ]
    fo, bo = pl.pallas_call(
        functools.partial(kernel, ny, npipe, ct),
        out_shape=[jax.ShapeDtypeStruct((tok, width), bf)] * 2,
        in_specs=[vmem] * 8 + [hbm] * 3,
        out_specs=[vmem] * 2,
        scratch_shapes=scratch,
        compiler_params=pltpu.CompilerParams(
            collective_id=0, has_side_effects=True, vmem_limit_bytes=56 << 20
        ),
    )(
        fwd_state[0], bwd_state[0], saved_input[0], fwd_route.reshape(2, tok), bwd_route.reshape(2, tok),
        fwd_gate[0], bwd_gate[0], norm_gain, w_gate[0], w_up[0], w_down[0],
    )
    return fo[None], bo[None]


def solution(mesh):
    placed = (
        P("pipe", "expert", None),
        P("pipe", "expert", None),
        P("pipe", None, "expert", None),
        P("pipe", None, "expert", None),
        P("pipe", None, "expert", None),
        P("pipe", None, "expert"),
        P("pipe", None, "expert"),
        P("pipe", None, "expert"),
        P("pipe", None, "expert"),
        P("pipe", "expert", None),
        P("pipe", None),
    )
    return jax.shard_map(
        functools.partial(local, mesh.shape["expert"], mesh.shape["pipe"]),
        mesh=mesh,
        in_specs=placed,
        out_specs=(P("pipe", "expert", None), P("pipe", "expert", None)),
        check_vma=False,
    )
```

```python
import functools

import jax
import jax.numpy as jnp
from jax import lax
from jax.experimental import pallas as pl
from jax.experimental.pallas import tpu as pltpu
from jax.sharding import PartitionSpec as P

EPS = 1e-06
NX = 4
PAIR = 2
SLOT = 8
BLK = 2 * SLOT
NT = (((1,), (1,)), ((), ()))


def dot(a, b):
    return jnp.dot(a, b, preferred_element_type=jnp.float32)


def dot_nt(a, b):
    return lax.dot_general(a, b, NT, preferred_element_type=jnp.float32)


def slots_of(route):
    tok = route.shape[0]
    lane = lax.broadcasted_iota(jnp.int32, (tok, 128), 1)
    hits = jnp.where(lane == route, 1.0, 0.0)
    row_i = lax.broadcasted_iota(jnp.int32, (tok, tok), 0)
    col_i = lax.broadcasted_iota(jnp.int32, (tok, tok), 1)
    lower = jnp.where(col_i < row_i, 1.0, 0.0)
    before = dot(lower.astype(jnp.bfloat16), hits.astype(jnp.bfloat16))
    return jnp.sum(before * hits, axis=1, keepdims=True).astype(jnp.int32)


def as_row(col):
    tok = col.shape[0]
    row_i = lax.broadcasted_iota(jnp.int32, (tok, tok), 0)
    col_i = lax.broadcasted_iota(jnp.int32, (tok, tok), 1)
    return jnp.sum(jnp.where(row_i == col_i, col, 0), axis=0, keepdims=True)


def as_col(row):
    tok = row.shape[1]
    row_i = lax.broadcasted_iota(jnp.int32, (tok, tok), 0)
    col_i = lax.broadcasted_iota(jnp.int32, (tok, tok), 1)
    return jnp.sum(jnp.where(row_i == col_i, row, jnp.zeros_like(row)), axis=1, keepdims=True)


def place(route, slot, rows, shift):
    target = as_row(route * BLK + (slot + shift))
    sub = lax.broadcasted_iota(jnp.int32, (rows, route.shape[0]), 0)
    return jnp.where(sub == target, 1.0, 0.0).astype(jnp.bfloat16)


def pick(route, slot, expert_of, shift):
    lane = lax.broadcasted_iota(jnp.int32, (route.shape[0], expert_of.shape[1]), 1)
    mine = (lane % BLK == slot + shift) & (expert_of == route)
    return jnp.where(mine, 1.0, 0.0).astype(jnp.bfloat16)


def kernel(
    ny, npipe, ct,
    fs, bs, sv, fr, br, fg, bg, gain, wg, wu, wd,
    res,
    wgu, wdn, mm, rows_in, dd, gs, dh, hs, ab, po, xs, xr, rs, rr, acc, dn, xf, xb, yf, yb,
    l_sem, ws_sem, wr_sem, ds_sem, dr_sem, es_sem, er_sem, cs_sem, cr_sem, rs_sem, rr_sem, ss_sem, sr_sem,
):
    width = wd.shape[1]
    hid = wd.shape[0]
    tok = fs.shape[0]
    half = width // 2
    tiles = half // ct
    groups = ny // PAIR
    ns = ny // PAIR
    me = lax.axis_index("expert")
    pipe = lax.axis_index("pipe")
    y, x = me // NX, me % NX
    sg = 1 - 2 * (y % 2)
    core = pipe % 2
    p_next = (pipe + 1) % npipe
    p_prev = (pipe + npipe - 1) % npipe
    mesh_id = pl.DeviceIdType.MESH

    def at_row(row):
        return (pipe, ((row + ny) % ny) * NX + x)

    def at_col(col):
        return (pipe, y * NX + (col + NX) % NX)

    def source_row(j):
        return (y - sg * j + ny) % ny

    def target_row(j):
        return (y + (sg * j if j % 2 == 0 else -sg * j) + ny) % ny

    partner = at_row(y + sg)
    across = at_col(x + 2)
    taker = at_col(x + 3 + 2 * core)

    loads = [
        pltpu.make_async_copy(wg, wgu.at[0, :, pl.ds(0, hid)], l_sem.at[0]),
        pltpu.make_async_copy(wu, wgu.at[0, :, pl.ds(hid, hid)], l_sem.at[1]),
        pltpu.make_async_copy(wd, wdn.at[pl.ds(0, hid)], l_sem.at[2]),
    ]
    for c in loads:
        c.start()

    barrier = pltpu.get_barrier_semaphore()
    peers = [at_row(y + k) for k in range(1, ny)] + [at_col(x + k) for k in range(1, NX)]
    peers += [(p_next, me), (p_prev, me)]
    for dev in peers:
        pl.semaphore_signal(barrier, inc=1, device_id=dev, device_id_type=mesh_id)

    def remote(src, dst, send, recv, dev):
        return pltpu.make_async_remote_copy(
            src_ref=src, dst_ref=dst, send_sem=send, recv_sem=recv,
            device_id=dev, device_id_type=mesh_id,
        )

    def part(q, i):
        if i < 4:
            return wgu.at[q, pl.ds(i * (width // 4), width // 4)]
        return wdn.at[pl.ds(q * hid + (i - 4) * (hid // 4), hid // 4)]

    to_partner = [remote(part(0, i), part(2, i), ws_sem.at[i], wr_sem.at[i], partner) for i in range(8)]
    to_taker = [
        remote(wgu.at[0], wgu.at[1], ws_sem.at[16], wr_sem.at[16], taker),
        remote(wdn.at[pl.ds(0, hid)], wdn.at[pl.ds(hid, hid)], ws_sem.at[17], wr_sem.at[17], taker),
    ]
    passed = [remote(part(2, i), part(3, i), ws_sem.at[8 + i], wr_sem.at[8 + i], taker) for i in range(7)]
    by_partner = remote(part(1, 7), part(3, 7), ws_sem.at[15], wr_sem.at[15], partner)

    far_first = list(range(ns - 1, 0, -1))

    def blk(ref, i):
        start = i * BLK if isinstance(i, int) else pl.multiple_of(i * BLK, BLK)
        return ref.at[pl.ds(start, BLK)]

    def send_copy(kind, j):
        return remote(
            blk(mm, kind * groups + target_row(j) // PAIR), blk(dd, kind * ny + j),
            ds_sem.at[kind, j], dr_sem.at[kind, j], at_row(target_row(j)),
        )

    def pass_copy(kind, j):
        return remote(
            blk(dd, kind * ny + j), blk(dd, kind * ny + ns + j),
            es_sem.at[kind, j], er_sem.at[kind, j], across,
        )

    def scatter(kind):
        for j in far_first:
            send_copy(kind, j).start()
        blk(dd, kind * ny)[...] = blk(mm, kind * groups + y // PAIR)[...]
        pass_copy(kind, 0).start()

    def scatter_pass(kind):
        for j in range(1, ns):
            send_copy(kind, j).wait_recv()
            pass_copy(kind, j).start()

    def scatter_end(kind):
        for j in range(ns):
            pass_copy(kind, j).wait_recv()

    def norm_scale(raw):
        return lax.rsqrt(jnp.mean(raw * raw, axis=-1, keepdims=True) + EPS)

    g = gain[...]
    routes_f = [as_col(fr[pl.ds(t, 1), :]) for t in range(2)]
    routes_b = [as_col(br[pl.ds(t, 1), :]) for t in range(2)]
    slots_f = [slots_of(r) for r in routes_f]
    slots_b = [slots_of(r) for r in routes_b]
    gates_f = [as_col(fg[pl.ds(t, 1), :]) for t in range(2)]
    gates_b = [as_col(bg[pl.ds(t, 1), :]) for t in range(2)]

    def fill(kind, route, slot, values):
        rows_in[...] = values.astype(jnp.bfloat16)
        lo = place(route, slot, groups * BLK, 0)
        hi = place(route, slot, groups * BLK, SLOT)

        def tile(i, carry):
            start = pl.multiple_of(i * ct, ct)
            cols = pl.ds(start, ct)
            cols2 = pl.ds(pl.multiple_of(half + start, 128), ct)
            both = dot(lo, rows_in[:, cols]) + dot(hi, rows_in[:, cols2])
            mm[pl.ds(kind * groups * BLK, groups * BLK), cols] = both.astype(jnp.bfloat16)
            return carry

        lax.fori_loop(0, tiles, tile, 0)

    def fill_tokens(kind, t, state):
        raw = state[...].astype(jnp.float32)
        fill(kind, routes_f[t], slots_f[t], raw * norm_scale(raw) * g)

    def fill_grads(kind, t, state):
        fill(kind, routes_b[t], slots_b[t], gates_b[t] * state[...].astype(jnp.float32))

    def fill_saved(kind, t):
        raw = sv[t].astype(jnp.float32)
        scale = norm_scale(raw)
        fill(kind, routes_b[t], slots_b[t], raw * scale * g)
        return scale

    fill_tokens(0, 0, fs)
    pl.semaphore_wait(barrier, len(peers))
    loads[0].wait()
    loads[1].wait()
    to_taker[0].start()
    scatter(0)
    to_partner[0].start()
    fill_grads(2, 0, bs)
    scatter(2)
    b_scale = [fill_saved(1, 0)]
    scatter(1)
    loads[2].wait()
    for c in to_partner[1:]:
        c.start()
    b_scale.append(fill_saved(3, 1))
    for kind in (0, 2, 1):
        scatter_pass(kind)
    to_taker[1].start()
    for j in far_first:
        send_copy(3, j).start()
    blk(dd, 3 * ny)[...] = blk(mm, 3 * groups + y // PAIR)[...]

    def folded(kind, count, product, w_lo, w_hi):
        a = dd[pl.ds(kind * ny * BLK, count * ny * BLK)]
        lo = product(a, w_lo).reshape(count * ny, BLK, -1)[:, :SLOT]
        hi = product(a, w_hi).reshape(count * ny, BLK, -1)[:, SLOT:]
        return lo + hi

    def through_up(q, kind, count, at):
        gs[q, pl.ds(at * ny, count * ny)] = folded(
            kind, count, dot, wgu[q, pl.ds(0, half)], wgu[q, pl.ds(half, half)]
        )

    def through_down(q, kind, t):
        w_q = wdn.at[pl.ds(q * hid, hid)]
        dh[q, pl.ds(t * ny, ny)] = folded(
            kind, 1, dot_nt, w_q[:, pl.ds(0, half)], w_q[:, pl.ds(half, half)]
        )

    def into_hidden(q):
        through_up(q, 0, 2, 0)
        through_down(q, 2, 0)

    for i in range(2):
        to_partner[i].wait_recv()
        passed[i].start()
    for kind in (0, 2, 1):
        scatter_end(kind)
    into_hidden(0)
    for i in range(2, 4):
        to_partner[i].wait_recv()
        passed[i].start()
    for c in to_taker:
        c.wait_recv()
    by_partner.start()
    into_hidden(1)
    for i in range(4, 7):
        to_partner[i].wait_recv()
        passed[i].start()
    to_partner[7].wait_recv()
    into_hidden(2)

    rows = ny * SLOT

    def put_out(c, i, lo, hi):
        cols = pl.ds(pl.multiple_of(i * ct, ct), ct)
        both = jnp.concatenate([lo.reshape(ny, SLOT, ct), hi.reshape(ny, SLOT, ct)], axis=1)
        po[c % 2, :, :, cols] = both[:ns]
        xs[c, :, :, cols] = both[ns:].astype(jnp.bfloat16)

    def hidden_f(q, at):
        f = gs[q, pl.ds(at * ny, ny)].reshape(rows, 2 * hid)
        gated, upped = f[:, :hid], f[:, hid:]
        hidden = gated * jax.nn.sigmoid(gated) * upped
        hs[:, pl.ds(q * hid, hid)] = hidden.astype(jnp.bfloat16)

    def hidden_b(q, t, at):
        b = gs[q, pl.ds(at * ny, ny)].reshape(rows, 2 * hid)
        gated, upped = b[:, :hid], b[:, hid:]
        dhid = dh[q, pl.ds(t * ny, ny)].reshape(rows, hid)
        s = jax.nn.sigmoid(gated)
        da = dhid * upped * s * (1.0 + gated * (1.0 - s))
        db = dhid * gated * s
        ab[q, :, pl.ds(0, hid)] = da.astype(jnp.bfloat16)
        ab[q, :, pl.ds(hid, hid)] = db.astype(jnp.bfloat16)

    def part_f(qs, start):
        units = pl.ds(qs[0] * hid, len(qs) * hid)
        return dot(hs[:, units], wdn[units, pl.ds(start, ct)])

    def part_b(qs, start):
        terms = [dot_nt(ab[q], wgu[q, pl.ds(start, ct), :]) for q in qs]
        return functools.reduce(lambda a, b: a + b, terms)

    def early(kind, product, qs):
        def tile(i, carry):
            for w in both_halves(i)[1]:
                acc[kind, :, w] = product(qs, w.start)
            return carry

        lax.fori_loop(0, tiles, tile, 0)

    def out(c, product, qs, with_early):
        def tile(i, carry):
            sums = []
            for w in both_halves(i)[1]:
                value = product(qs, w.start)
                sums.append(value + acc[c % 2, :, w] if with_early else value)
            put_out(c, i, *sums)
            return carry

        lax.fori_loop(0, tiles, tile, 0)
        half_start(c)

    def both_halves(i):
        start = pl.multiple_of(i * ct, ct)
        return pl.ds(start, ct), (pl.ds(start, ct), pl.ds(pl.multiple_of(half + start, 128), ct))

    def half_copy(c, j):
        return remote(xs.at[c, j], xr.at[c, j], cs_sem.at[c, j], cr_sem.at[c, j], across)

    def back_copy(c, j):
        return remote(rs.at[c, j], rr.at[c, j], rs_sem.at[c, j], rr_sem.at[c, j], at_row(source_row(j)))

    def half_start(c):
        for j in far_first + [0]:
            half_copy(c, j).start()

    def back_start(c):
        for j in far_first + [0]:
            half_copy(c, j).wait_recv()
            (rs if j else rr)[c, j] = (po[c % 2, j] + xr[c, j].astype(jnp.float32)).astype(jnp.bfloat16)
            if j:
                back_copy(c, j).start()

    def back_wait(c):
        for j in range(1, ns):
            back_copy(c, j).wait_recv()

    jb = lax.broadcasted_iota(jnp.int32, (tok, ns * BLK), 1) // BLK
    step = jnp.where(jb % 2 == 0, jb, -jb) * sg
    expert_of = ((y + step + ny) % ny) // PAIR

    def finish_f(t, old, out):
        sel = [pick(routes_f[t], slots_f[t], expert_of, shift) for shift in (0, SLOT)]

        def tile(i, carry):
            cols, wide = both_halves(i)
            back = rr[2 * t, :, :, cols].reshape(ns * BLK, ct)
            for s, w in zip(sel, wide):
                new = old[:, w].astype(jnp.float32) + gates_f[t] * dot(s, back)
                out[pl.ds(0, tok), w] = new.astype(jnp.bfloat16)
            return carry

        lax.fori_loop(0, tiles, tile, 0)

    def finish_b(t, old, out):
        sel = [pick(routes_b[t], slots_b[t], expert_of, shift) for shift in (0, SLOT)]

        def tile(i, total):
            cols, wide = both_halves(i)
            back = rr[2 * t + 1, :, :, cols].reshape(ns * BLK, ct)
            for s, w in zip(sel, wide):
                weighted = gain[:, w] * dot(s, back)
                dn[:, w] = weighted
                total = total + jnp.sum(
                    sv[t, :, w].astype(jnp.float32) * weighted, axis=-1, keepdims=True
                )
            return total

        total = lax.fori_loop(0, tiles, tile, jnp.zeros((tok, 1), jnp.float32))
        r = b_scale[t]
        factor = r * r * r * (total * (1.0 / width))

        def tile2(i, carry):
            for w in both_halves(i)[1]:
                saved = sv[t, :, w].astype(jnp.float32)
                dx = old[:, w].astype(jnp.float32) + (r * dn[:, w] - saved * factor)
                out[pl.ds(0, tok), w] = dx.astype(jnp.bfloat16)
            return carry

        lax.fori_loop(0, tiles, tile2, 0)

    some, last = list(range(NX - 1)), [NX - 1]
    for q in some:
        hidden_f(q, 0)
        hidden_b(q, 0, 1)
    early(0, part_f, some)
    early(1, part_b, some)
    for c in passed + [by_partner]:
        c.wait_recv()
    into_hidden(NX - 1)
    hidden_f(NX - 1, 0)
    out(0, part_f, last, True)
    hidden_b(NX - 1, 0, 1)
    out(1, part_b, last, True)
    back_start(0)
    back_start(1)
    pass_copy(3, 0).start()
    scatter_pass(3)

    sf = remote(xf, yf, ss_sem.at[0], sr_sem.at[0], (p_next, me))
    sb = remote(xb, yb, ss_sem.at[1], sr_sem.at[1], (p_prev, me))
    back_wait(0)
    finish_f(0, fs, xf)
    sf.start()
    back_wait(1)
    finish_b(0, bs, xb)
    sb.start()
    scatter_end(3)
    for q in range(NX):
        through_up(q, 3, 1, 2)
    keep_f = jnp.where(pipe > 0, 1.0, 0.0)
    keep_b = jnp.where(pipe < npipe - 1, 1.0, 0.0)
    f_old = yf.at[pl.ds(0, tok)]
    b_old = yb.at[pl.ds(0, tok)]

    sf.wait_recv()
    yf[...] = (yf[...].astype(jnp.float32) * keep_f).astype(jnp.bfloat16)
    fill_tokens(4, 1, f_old)
    scatter(4)
    sb.wait_recv()
    yb[...] = (yb[...].astype(jnp.float32) * keep_b).astype(jnp.bfloat16)
    fill_grads(5, 1, b_old)
    scatter(5)
    scatter_pass(4)
    scatter_pass(5)
    scatter_end(4)
    for q in range(NX):
        through_up(q, 4, 1, 3)
        hidden_f(q, 3)
    out(2, part_f, some + last, False)
    scatter_end(5)
    for q in range(NX):
        through_down(q, 5, 1)
        hidden_b(q, 1, 2)
    out(3, part_b, some + last, False)
    back_start(2)
    back_start(3)
    back_wait(2)
    finish_f(1, f_old, res.at[0])
    back_wait(3)
    finish_b(1, b_old, res.at[1])

    for c in to_partner + to_taker + passed + [by_partner]:
        c.wait_send()
    for kind in range(6):
        for j in range(ns):
            if j:
                send_copy(kind, j).wait_send()
            pass_copy(kind, j).wait_send()
    for c in range(4):
        for j in range(ns):
            half_copy(c, j).wait_send()
            if j:
                back_copy(c, j).wait_send()
    sf.wait_send()
    sb.wait_send()


def local(
    n_expert, npipe, fwd_state, bwd_state, saved_input, fwd_route, bwd_route, fwd_gate, bwd_gate,
    w_gate, w_up, w_down, norm_gain,
):
    ny = n_expert // NX
    experts = ny // PAIR
    tok, width = fwd_state.shape[1:]
    hid = w_down.shape[1]
    ct = 256
    pad = -(-tok // 16) * 16
    bf, f32 = jnp.bfloat16, jnp.float32
    vmem = pl.BlockSpec(memory_space=pltpu.VMEM)
    hbm = pl.BlockSpec(memory_space=pl.ANY)
    ns = ny // PAIR
    scratch = [
        pltpu.VMEM((NX, width, 2 * hid), bf),
        pltpu.VMEM((NX * hid, width), bf),
        pltpu.VMEM((6 * experts * BLK, width // 2), bf),
        pltpu.VMEM((tok, width), bf),
        pltpu.VMEM((6 * ny * BLK, width // 2), bf),
        pltpu.VMEM((NX, 4 * ny, SLOT, 2 * hid), f32),
        pltpu.VMEM((NX, 2 * ny, SLOT, hid), f32),
        pltpu.VMEM((ny * SLOT, NX * hid), bf),
        pltpu.VMEM((NX, ny * SLOT, 2 * hid), bf),
        pltpu.VMEM((2, ns, BLK, width // 2), f32),
    ]
    scratch += [pltpu.VMEM((4, ns, BLK, width // 2), bf)] * 4
    scratch += [
        pltpu.VMEM((2, ny * SLOT, width), f32),
        pltpu.VMEM((tok, width), f32),
        pltpu.VMEM((pad, width), bf),
        pltpu.VMEM((pad, width), bf),
        pltpu.VMEM((pad, width), bf),
        pltpu.VMEM((pad, width), bf),
    ]
    scratch += [
        pltpu.SemaphoreType.DMA(shape)
        for shape in (
            (3,), (18,), (18,), (6, ns), (6, ns), (6, ns), (6, ns), (4, ns), (4, ns), (4, ns), (4, ns),
            (2,), (2,),
        )
    ]
    res = pl.pallas_call(
        functools.partial(kernel, ny, npipe, ct),
        out_shape=jax.ShapeDtypeStruct((2, tok, width), bf),
        in_specs=[vmem] * 8 + [hbm] * 3,
        out_specs=vmem,
        scratch_shapes=scratch,
        compiler_params=pltpu.CompilerParams(
            collective_id=0, has_side_effects=True, vmem_limit_bytes=56 << 20
        ),
    )(
        fwd_state[0], bwd_state[0], saved_input[0], fwd_route.reshape(2, tok), bwd_route.reshape(2, tok),
        fwd_gate[0], bwd_gate[0], norm_gain, w_gate[0], w_up[0], w_down[0],
    )
    return res[0:1], res[1:2]


def solution(mesh):
    placed = (
        P("pipe", "expert", None),
        P("pipe", "expert", None),
        P("pipe", None, "expert", None),
        P("pipe", None, "expert", None),
        P("pipe", None, "expert", None),
        P("pipe", None, "expert"),
        P("pipe", None, "expert"),
        P("pipe", None, "expert"),
        P("pipe", None, "expert"),
        P("pipe", "expert", None),
        P("pipe", None),
    )
    return jax.shard_map(
        functools.partial(local, mesh.shape["expert"], mesh.shape["pipe"]),
        mesh=mesh,
        in_specs=placed,
        out_specs=(P("pipe", "expert", None), P("pipe", "expert", None)),
        check_vma=False,
    )
```

```python
import functools

import jax
import jax.numpy as jnp
from jax import lax
from jax.experimental import pallas as pl
from jax.experimental.pallas import tpu as pltpu
from jax.sharding import PartitionSpec as P

EPS = 1e-06
NX = 4
PAIR = 2
SLOT = 8
BLK = 2 * SLOT
NT = (((1,), (1,)), ((), ()))


def dot(a, b):
    return jnp.dot(a, b, preferred_element_type=jnp.float32)


def dot_nt(a, b):
    return lax.dot_general(a, b, NT, preferred_element_type=jnp.float32)


def slots_of(route):
    tok = route.shape[0]
    lane = lax.broadcasted_iota(jnp.int32, (tok, 128), 1)
    hits = jnp.where(lane == route, 1.0, 0.0)
    row_i = lax.broadcasted_iota(jnp.int32, (tok, tok), 0)
    col_i = lax.broadcasted_iota(jnp.int32, (tok, tok), 1)
    lower = jnp.where(col_i < row_i, 1.0, 0.0)
    before = dot(lower.astype(jnp.bfloat16), hits.astype(jnp.bfloat16))
    return jnp.sum(before * hits, axis=1, keepdims=True).astype(jnp.int32)


def as_row(col):
    tok = col.shape[0]
    row_i = lax.broadcasted_iota(jnp.int32, (tok, tok), 0)
    col_i = lax.broadcasted_iota(jnp.int32, (tok, tok), 1)
    return jnp.sum(jnp.where(row_i == col_i, col, 0), axis=0, keepdims=True)


def as_col(row):
    tok = row.shape[1]
    row_i = lax.broadcasted_iota(jnp.int32, (tok, tok), 0)
    col_i = lax.broadcasted_iota(jnp.int32, (tok, tok), 1)
    return jnp.sum(jnp.where(row_i == col_i, row, jnp.zeros_like(row)), axis=1, keepdims=True)


def place(route, slot, rows, shift):
    target = as_row(route * BLK + (slot + shift))
    sub = lax.broadcasted_iota(jnp.int32, (rows, route.shape[0]), 0)
    return jnp.where(sub == target, 1.0, 0.0).astype(jnp.bfloat16)


def pick(route, slot, expert_of, shift):
    lane = lax.broadcasted_iota(jnp.int32, (route.shape[0], expert_of.shape[1]), 1)
    mine = (lane % BLK == slot + shift) & (expert_of == route)
    return jnp.where(mine, 1.0, 0.0).astype(jnp.bfloat16)


def kernel(
    ny, npipe, ct,
    fs, bs, sv, fr, br, fg, bg, gain, wg, wu, wd,
    res,
    wgu, wdn, mm, rows_in, dd, gs, dh, hs, ab, po, xs, xr, rs, rr, acc, dn, xf, xb, yf, yb,
    l_sem, ws_sem, wr_sem, ds_sem, dr_sem, es_sem, er_sem, cs_sem, cr_sem, rs_sem, rr_sem, ss_sem, sr_sem,
):
    width = wd.shape[1]
    hid = wd.shape[0]
    tok = fs.shape[0]
    half = width // 2
    tiles = half // ct
    groups = ny // PAIR
    ns = ny // PAIR
    me = lax.axis_index("expert")
    pipe = lax.axis_index("pipe")
    y, x = me // NX, me % NX
    sg = 1 - 2 * (y % 2)
    core = pipe % 2
    p_next = (pipe + 1) % npipe
    p_prev = (pipe + npipe - 1) % npipe
    mesh_id = pl.DeviceIdType.MESH

    def at_row(row):
        return (pipe, ((row + ny) % ny) * NX + x)

    def at_col(col):
        return (pipe, y * NX + (col + NX) % NX)

    def source_row(j):
        return (y - sg * j + ny) % ny

    def target_row(j):
        return (y + (sg * j if j % 2 == 0 else -sg * j) + ny) % ny

    partner = at_row(y + sg)
    across = at_col(x + 2)
    taker = at_col(x + 3 + 2 * core)

    loads = [
        pltpu.make_async_copy(wg, wgu.at[0, :, pl.ds(0, hid)], l_sem.at[0]),
        pltpu.make_async_copy(wu, wgu.at[0, :, pl.ds(hid, hid)], l_sem.at[1]),
        pltpu.make_async_copy(wd, wdn.at[pl.ds(0, hid)], l_sem.at[2]),
    ]
    for c in loads:
        c.start()

    barrier = pltpu.get_barrier_semaphore()
    peers = [at_row(y + k) for k in range(1, ny)] + [at_col(x + k) for k in range(1, NX)]
    peers += [(p_next, me), (p_prev, me)]
    for dev in peers:
        pl.semaphore_signal(barrier, inc=1, device_id=dev, device_id_type=mesh_id)

    def remote(src, dst, send, recv, dev):
        return pltpu.make_async_remote_copy(
            src_ref=src, dst_ref=dst, send_sem=send, recv_sem=recv,
            device_id=dev, device_id_type=mesh_id,
        )

    def part(q, i):
        if i < 4:
            return wgu.at[q, pl.ds(i * (width // 4), width // 4)]
        return wdn.at[pl.ds(q * hid + (i - 4) * (hid // 4), hid // 4)]

    to_partner = [remote(part(0, i), part(2, i), ws_sem.at[i], wr_sem.at[i], partner) for i in range(8)]
    to_taker = [
        remote(wgu.at[0], wgu.at[1], ws_sem.at[16], wr_sem.at[16], taker),
        remote(wdn.at[pl.ds(0, hid)], wdn.at[pl.ds(hid, hid)], ws_sem.at[17], wr_sem.at[17], taker),
    ]
    passed = [remote(part(2, i), part(3, i), ws_sem.at[8 + i], wr_sem.at[8 + i], taker) for i in range(7)]
    by_partner = remote(part(1, 7), part(3, 7), ws_sem.at[15], wr_sem.at[15], partner)

    far_first = list(range(ns - 1, 0, -1))

    def blk(ref, i):
        start = i * BLK if isinstance(i, int) else pl.multiple_of(i * BLK, BLK)
        return ref.at[pl.ds(start, BLK)]

    def send_copy(kind, j):
        return remote(
            blk(mm, kind * groups + target_row(j) // PAIR), blk(dd, kind * ny + j),
            ds_sem.at[kind, j], dr_sem.at[kind, j], at_row(target_row(j)),
        )

    def pass_copy(kind, j):
        return remote(
            blk(dd, kind * ny + j), blk(dd, kind * ny + ns + j),
            es_sem.at[kind, j], er_sem.at[kind, j], across,
        )

    def scatter(kind):
        for j in far_first:
            send_copy(kind, j).start()
        blk(dd, kind * ny)[...] = blk(mm, kind * groups + y // PAIR)[...]
        pass_copy(kind, 0).start()

    def scatter_pass(kind):
        for j in range(1, ns):
            send_copy(kind, j).wait_recv()
            pass_copy(kind, j).start()

    def scatter_end(kind):
        for j in range(ns):
            pass_copy(kind, j).wait_recv()

    def norm_scale(raw):
        return lax.rsqrt(jnp.mean(raw * raw, axis=-1, keepdims=True) + EPS)

    g = gain[...]
    routes_f = [as_col(fr[pl.ds(t, 1), :]) for t in range(2)]
    routes_b = [as_col(br[pl.ds(t, 1), :]) for t in range(2)]
    slots_f = [slots_of(r) for r in routes_f]
    slots_b = [slots_of(r) for r in routes_b]
    gates_f = [as_col(fg[pl.ds(t, 1), :]) for t in range(2)]
    gates_b = [as_col(bg[pl.ds(t, 1), :]) for t in range(2)]

    def fill(kind, route, slot, values):
        rows_in[...] = values.astype(jnp.bfloat16)
        lo = place(route, slot, groups * BLK, 0)
        hi = place(route, slot, groups * BLK, SLOT)

        def tile(i, carry):
            start = pl.multiple_of(i * ct, ct)
            cols = pl.ds(start, ct)
            cols2 = pl.ds(pl.multiple_of(half + start, 128), ct)
            both = dot(lo, rows_in[:, cols]) + dot(hi, rows_in[:, cols2])
            mm[pl.ds(kind * groups * BLK, groups * BLK), cols] = both.astype(jnp.bfloat16)
            return carry

        lax.fori_loop(0, tiles, tile, 0)

    def fill_tokens(kind, t, state):
        raw = state[...].astype(jnp.float32)
        fill(kind, routes_f[t], slots_f[t], raw * norm_scale(raw) * g)

    def fill_grads(kind, t, state):
        fill(kind, routes_b[t], slots_b[t], gates_b[t] * state[...].astype(jnp.float32))

    def fill_saved(kind, t):
        raw = sv[t].astype(jnp.float32)
        scale = norm_scale(raw)
        fill(kind, routes_b[t], slots_b[t], raw * scale * g)
        return scale

    fill_tokens(0, 0, fs)
    pl.semaphore_wait(barrier, len(peers))
    loads[0].wait()
    loads[1].wait()
    to_taker[0].start()
    scatter(0)
    to_partner[0].start()
    fill_grads(2, 0, bs)
    scatter(2)
    b_scale = [fill_saved(1, 0)]
    scatter(1)
    loads[2].wait()
    for c in to_partner[1:]:
        c.start()
    scatter_pass(0)
    to_taker[1].start()
    for kind in (2, 1):
        scatter_pass(kind)
    b_scale.append(fill_saved(3, 1))
    for j in far_first:
        send_copy(3, j).start()
    blk(dd, 3 * ny)[...] = blk(mm, 3 * groups + y // PAIR)[...]

    def folded(kind, count, product, w_lo, w_hi):
        a = dd[pl.ds(kind * ny * BLK, count * ny * BLK)]
        lo = product(a, w_lo).reshape(count * ny, BLK, -1)[:, :SLOT]
        hi = product(a, w_hi).reshape(count * ny, BLK, -1)[:, SLOT:]
        return lo + hi

    def through_up(q, kind, count, at):
        gs[q, pl.ds(at * ny, count * ny)] = folded(
            kind, count, dot, wgu[q, pl.ds(0, half)], wgu[q, pl.ds(half, half)]
        )

    def through_down(q, kind, t):
        w_q = wdn.at[pl.ds(q * hid, hid)]
        dh[q, pl.ds(t * ny, ny)] = folded(
            kind, 1, dot_nt, w_q[:, pl.ds(0, half)], w_q[:, pl.ds(half, half)]
        )

    def into_hidden(q):
        through_up(q, 0, 2, 0)
        through_down(q, 2, 0)

    for i in range(2):
        to_partner[i].wait_recv()
        passed[i].start()
    for kind in (0, 2, 1):
        scatter_end(kind)
    into_hidden(0)
    for i in range(2, 4):
        to_partner[i].wait_recv()
        passed[i].start()
    for c in to_taker:
        c.wait_recv()
    by_partner.start()
    into_hidden(1)
    for i in range(4, 7):
        to_partner[i].wait_recv()
        passed[i].start()
    to_partner[7].wait_recv()
    into_hidden(2)

    rows = ny * SLOT

    def put_out(c, i, lo, hi):
        cols = pl.ds(pl.multiple_of(i * ct, ct), ct)
        both = jnp.concatenate([lo.reshape(ny, SLOT, ct), hi.reshape(ny, SLOT, ct)], axis=1)
        po[c % 2, :, :, cols] = both[:ns]
        xs[c, :, :, cols] = both[ns:].astype(jnp.bfloat16)

    def hidden_f(q, at):
        f = gs[q, pl.ds(at * ny, ny)].reshape(rows, 2 * hid)
        gated, upped = f[:, :hid], f[:, hid:]
        hidden = gated * jax.nn.sigmoid(gated) * upped
        hs[:, pl.ds(q * hid, hid)] = hidden.astype(jnp.bfloat16)

    def hidden_b(q, t, at):
        b = gs[q, pl.ds(at * ny, ny)].reshape(rows, 2 * hid)
        gated, upped = b[:, :hid], b[:, hid:]
        dhid = dh[q, pl.ds(t * ny, ny)].reshape(rows, hid)
        s = jax.nn.sigmoid(gated)
        da = dhid * upped * s * (1.0 + gated * (1.0 - s))
        db = dhid * gated * s
        ab[q, :, pl.ds(0, hid)] = da.astype(jnp.bfloat16)
        ab[q, :, pl.ds(hid, hid)] = db.astype(jnp.bfloat16)

    def part_f(qs, start):
        units = pl.ds(qs[0] * hid, len(qs) * hid)
        return dot(hs[:, units], wdn[units, pl.ds(start, ct)])

    def part_b(qs, start):
        terms = [dot_nt(ab[q], wgu[q, pl.ds(start, ct), :]) for q in qs]
        return functools.reduce(lambda a, b: a + b, terms)

    def early(kind, product, qs):
        def tile(i, carry):
            for w in both_halves(i)[1]:
                acc[kind, :, w] = product(qs, w.start)
            return carry

        lax.fori_loop(0, tiles, tile, 0)

    def out(c, product, qs, with_early):
        def tile(i, carry):
            sums = []
            for w in both_halves(i)[1]:
                value = product(qs, w.start)
                sums.append(value + acc[c % 2, :, w] if with_early else value)
            put_out(c, i, *sums)
            return carry

        lax.fori_loop(0, tiles, tile, 0)
        half_start(c)

    def both_halves(i):
        start = pl.multiple_of(i * ct, ct)
        return pl.ds(start, ct), (pl.ds(start, ct), pl.ds(pl.multiple_of(half + start, 128), ct))

    def half_copy(c, j):
        return remote(xs.at[c, j], xr.at[c, j], cs_sem.at[c, j], cr_sem.at[c, j], across)

    def back_copy(c, j):
        return remote(rs.at[c, j], rr.at[c, j], rs_sem.at[c, j], rr_sem.at[c, j], at_row(source_row(j)))

    def half_start(c):
        for j in far_first + [0]:
            half_copy(c, j).start()

    def back_start(c):
        for j in far_first + [0]:
            half_copy(c, j).wait_recv()
            (rs if j else rr)[c, j] = (po[c % 2, j] + xr[c, j].astype(jnp.float32)).astype(jnp.bfloat16)
            if j:
                back_copy(c, j).start()

    def back_wait(c):
        for j in range(1, ns):
            back_copy(c, j).wait_recv()

    jb = lax.broadcasted_iota(jnp.int32, (tok, ns * BLK), 1) // BLK
    step = jnp.where(jb % 2 == 0, jb, -jb) * sg
    expert_of = ((y + step + ny) % ny) // PAIR

    def finish_f(t, old, out):
        sel = [pick(routes_f[t], slots_f[t], expert_of, shift) for shift in (0, SLOT)]

        def tile(i, carry):
            cols, wide = both_halves(i)
            back = rr[2 * t, :, :, cols].reshape(ns * BLK, ct)
            for s, w in zip(sel, wide):
                new = old[:, w].astype(jnp.float32) + gates_f[t] * dot(s, back)
                out[pl.ds(0, tok), w] = new.astype(jnp.bfloat16)
            return carry

        lax.fori_loop(0, tiles, tile, 0)

    def finish_b(t, old, out):
        sel = [pick(routes_b[t], slots_b[t], expert_of, shift) for shift in (0, SLOT)]

        def tile(i, total):
            cols, wide = both_halves(i)
            back = rr[2 * t + 1, :, :, cols].reshape(ns * BLK, ct)
            for s, w in zip(sel, wide):
                weighted = gain[:, w] * dot(s, back)
                dn[:, w] = weighted
                total = total + jnp.sum(
                    sv[t, :, w].astype(jnp.float32) * weighted, axis=-1, keepdims=True
                )
            return total

        total = lax.fori_loop(0, tiles, tile, jnp.zeros((tok, 1), jnp.float32))
        r = b_scale[t]
        factor = r * r * r * (total * (1.0 / width))

        def tile2(i, carry):
            for w in both_halves(i)[1]:
                saved = sv[t, :, w].astype(jnp.float32)
                dx = old[:, w].astype(jnp.float32) + (r * dn[:, w] - saved * factor)
                out[pl.ds(0, tok), w] = dx.astype(jnp.bfloat16)
            return carry

        lax.fori_loop(0, tiles, tile2, 0)

    some, last = list(range(NX - 1)), [NX - 1]
    for q in some:
        hidden_f(q, 0)
        hidden_b(q, 0, 1)
    early(0, part_f, some)
    early(1, part_b, some)
    for c in passed + [by_partner]:
        c.wait_recv()
    into_hidden(NX - 1)
    hidden_f(NX - 1, 0)
    out(0, part_f, last, True)
    hidden_b(NX - 1, 0, 1)
    out(1, part_b, last, True)
    back_start(0)
    back_start(1)
    pass_copy(3, 0).start()
    scatter_pass(3)

    sf = remote(xf, yf, ss_sem.at[0], sr_sem.at[0], (p_next, me))
    sb = remote(xb, yb, ss_sem.at[1], sr_sem.at[1], (p_prev, me))
    back_wait(0)
    finish_f(0, fs, xf)
    sf.start()
    back_wait(1)
    finish_b(0, bs, xb)
    sb.start()
    scatter_end(3)
    for q in range(NX):
        through_up(q, 3, 1, 2)
    keep_f = jnp.where(pipe > 0, 1.0, 0.0)
    keep_b = jnp.where(pipe < npipe - 1, 1.0, 0.0)
    f_old = yf.at[pl.ds(0, tok)]
    b_old = yb.at[pl.ds(0, tok)]

    sf.wait_recv()
    yf[...] = (yf[...].astype(jnp.float32) * keep_f).astype(jnp.bfloat16)
    fill_tokens(4, 1, f_old)
    scatter(4)
    sb.wait_recv()
    yb[...] = (yb[...].astype(jnp.float32) * keep_b).astype(jnp.bfloat16)
    fill_grads(5, 1, b_old)
    scatter(5)
    scatter_pass(4)
    scatter_pass(5)
    scatter_end(4)
    for q in range(NX):
        through_up(q, 4, 1, 3)
        hidden_f(q, 3)
    out(2, part_f, some + last, False)
    scatter_end(5)
    for q in range(NX):
        through_down(q, 5, 1)
        hidden_b(q, 1, 2)
    out(3, part_b, some + last, False)
    back_start(2)
    back_start(3)
    back_wait(2)
    finish_f(1, f_old, res.at[0])
    back_wait(3)
    finish_b(1, b_old, res.at[1])

    for c in to_partner + to_taker + passed + [by_partner]:
        c.wait_send()
    for kind in range(6):
        for j in range(ns):
            if j:
                send_copy(kind, j).wait_send()
            pass_copy(kind, j).wait_send()
    for c in range(4):
        for j in range(ns):
            half_copy(c, j).wait_send()
            if j:
                back_copy(c, j).wait_send()
    sf.wait_send()
    sb.wait_send()


def local(
    n_expert, npipe, fwd_state, bwd_state, saved_input, fwd_route, bwd_route, fwd_gate, bwd_gate,
    w_gate, w_up, w_down, norm_gain,
):
    ny = n_expert // NX
    experts = ny // PAIR
    tok, width = fwd_state.shape[1:]
    hid = w_down.shape[1]
    ct = 256
    pad = -(-tok // 16) * 16
    bf, f32 = jnp.bfloat16, jnp.float32
    vmem = pl.BlockSpec(memory_space=pltpu.VMEM)
    hbm = pl.BlockSpec(memory_space=pl.ANY)
    ns = ny // PAIR
    scratch = [
        pltpu.VMEM((NX, width, 2 * hid), bf),
        pltpu.VMEM((NX * hid, width), bf),
        pltpu.VMEM((6 * experts * BLK, width // 2), bf),
        pltpu.VMEM((tok, width), bf),
        pltpu.VMEM((6 * ny * BLK, width // 2), bf),
        pltpu.VMEM((NX, 4 * ny, SLOT, 2 * hid), f32),
        pltpu.VMEM((NX, 2 * ny, SLOT, hid), f32),
        pltpu.VMEM((ny * SLOT, NX * hid), bf),
        pltpu.VMEM((NX, ny * SLOT, 2 * hid), bf),
        pltpu.VMEM((2, ns, BLK, width // 2), f32),
    ]
    scratch += [pltpu.VMEM((4, ns, BLK, width // 2), bf)] * 4
    scratch += [
        pltpu.VMEM((2, ny * SLOT, width), f32),
        pltpu.VMEM((tok, width), f32),
        pltpu.VMEM((pad, width), bf),
        pltpu.VMEM((pad, width), bf),
        pltpu.VMEM((pad, width), bf),
        pltpu.VMEM((pad, width), bf),
    ]
    scratch += [
        pltpu.SemaphoreType.DMA(shape)
        for shape in (
            (3,), (18,), (18,), (6, ns), (6, ns), (6, ns), (6, ns), (4, ns), (4, ns), (4, ns), (4, ns),
            (2,), (2,),
        )
    ]
    res = pl.pallas_call(
        functools.partial(kernel, ny, npipe, ct),
        out_shape=jax.ShapeDtypeStruct((2, tok, width), bf),
        in_specs=[vmem] * 8 + [hbm] * 3,
        out_specs=vmem,
        scratch_shapes=scratch,
        compiler_params=pltpu.CompilerParams(
            collective_id=0, has_side_effects=True, vmem_limit_bytes=56 << 20
        ),
    )(
        fwd_state[0], bwd_state[0], saved_input[0], fwd_route.reshape(2, tok), bwd_route.reshape(2, tok),
        fwd_gate[0], bwd_gate[0], norm_gain, w_gate[0], w_up[0], w_down[0],
    )
    return res[0:1], res[1:2]


def solution(mesh):
    placed = (
        P("pipe", "expert", None),
        P("pipe", "expert", None),
        P("pipe", None, "expert", None),
        P("pipe", None, "expert", None),
        P("pipe", None, "expert", None),
        P("pipe", None, "expert"),
        P("pipe", None, "expert"),
        P("pipe", None, "expert"),
        P("pipe", None, "expert"),
        P("pipe", "expert", None),
        P("pipe", None),
    )
    return jax.shard_map(
        functools.partial(local, mesh.shape["expert"], mesh.shape["pipe"]),
        mesh=mesh,
        in_specs=placed,
        out_specs=(P("pipe", "expert", None), P("pipe", "expert", None)),
        check_vma=False,
    )
```
